128 devices in a mesh: band: 4 (over x), pts: 32 (over z, y, core).
Axes of the slice: x: 4, y: 4, z: 4, core: 2. Of those that a mesh axis runs over, the one named last changes fastest.
Arguments:
- spectra: float32 [16, 36, 36, 4096], P(None, 'band', None, 'pts'), may hold values from 0.05 to 1
- currents: float32 [2, 3, 16, 4096], P(None, None, 'band', 'pts'), may hold values from -4 to 4
- bathymetry: float32 [16, 4096], P('band', 'pts'), may hold values from 10 to 4000
- sea_mask: int32 [16, 4096], P('band', 'pts'), may hold values 0 or 1
Outputs:
- spectra_out: float32 [16, 36, 36, 4096], P(None, 'band', None, 'pts')
The draws below stay inside these ranges and needn't reach their ends.
Inputs may be any that keep to these rules, and one draw needn't show every extreme that they name: `sea_mask`: 1 marks a sea point, 0 land or ice.
All inputs are finite; a program needn't handle non-finite values. No bound on the sum of `sea_mask` on one device may be relied on, other than what follows from the above.
Results may differ from the reference program's by a relative error of at most 0.0001.
Values sent between devices are 32-bit elements; how exact they have to be, the bound alone decides.
No kernel may reach another device: no remote copies, remote signals or barrier semaphores. Data moves between devices by JAX's collectives and lax.ppermute only.
A program may use at most 192 MiB of HBM per device.

```python
import math
import jax
import jax.numpy as jnp
from jax import lax

ND = 36
NF = 36
SUBSTEPS = 2
NY = 16
NX = 4096
N_PTS = 32


def place_ends(drawn, own_key, smallest, top_value):
    longest = drawn.shape.index(max(drawn.shape))
    spots = []
    for shift in (0, 1):
        where = [jax.random.randint(jax.random.fold_in(own_key, axis), (), 0, length) for axis, length in enumerate(drawn.shape)]
        where[longest] = (where[longest] + shift) % drawn.shape[longest]
        spots.append(tuple(where))
    return drawn.at[spots[0]].set(smallest).at[spots[1]].set(top_value)


def block_levels(own_key, extent, pieces, least, top_value):
    def one(axis_at, shards_of):
        draws = jax.random.uniform(jax.random.fold_in(jax.random.fold_in(own_key, 6), axis_at), (shards_of,), jnp.float32, least / len(pieces), top_value / len(pieces))
        return jnp.repeat(jnp.exp(draws), extent[axis_at] // shards_of).reshape((-1,) + (1,) * (len(extent) - axis_at - 1))

    level = one(*pieces[0])
    for cut in pieces[1:]:
        level = level * one(*cut)
    return level


def normal_values(stream_key, dims, width, reach, shards=(), kind=jnp.bfloat16):
    result = width * jax.random.normal(stream_key, dims, jnp.float32)
    if shards:
        result = result * block_levels(stream_key, dims, shards, -0.22, 0.18)
    return jnp.clip(result, -reach, reach).astype(kind)


def setup_inputs(seed: int = 0) -> dict:
    key_of = jax.random.split(jax.random.key(seed), 5)
    return {
        "spectra": jnp.clip(jnp.exp(math.log(1.0) - 2.9957323 * jax.random.uniform(key_of[0], (NY, NF, ND, NX), jnp.float32) ** block_levels(key_of[0], (NY, NF, ND, NX), ((1, 4), (3, 32)), -0.2, 0.2)), 0.05, 1.0),
        "currents": normal_values(key_of[1], (SUBSTEPS, 3, NY, NX), 0.5, 4.0, ((2, 4), (3, 32)), jnp.float32),
        "bathymetry": jnp.clip(jnp.exp(math.log(4000.0) - 5.9914645 * jax.random.uniform(key_of[2], (NY, NX), jnp.float32) ** block_levels(key_of[2], (NY, NX), ((0, 4), (1, 32)), -0.2, 0.2)), 10.0, 4000.0),
        "sea_mask": place_ends((jax.random.randint(key_of[3], (NY, NX), 0, 10) < 7).astype(jnp.int32), jax.random.fold_in(key_of[3], 1), 0, 1),
    }


GRAVITY = 9.81
COURANT = 0.02
DISSIPATION = 1.0
MOMENT_FLOOR = 0.01
FREQ_FIRST = 0.035
FREQ_STEP = 1.1
BAND_WIDTH = 0.0955

def celerity_one(frequency, water_depth):
    angular = 2.0 * math.pi * frequency
    height = water_depth[:, None, :]
    deep_wavenumber = angular * angular / GRAVITY
    wavenumber = deep_wavenumber / jnp.sqrt(jnp.tanh(deep_wavenumber * height))
    scaled_depth = 2.0 * wavenumber * height
    depth_ratio = 2.0 * scaled_depth * jnp.exp(-scaled_depth) / (1.0 - jnp.exp(-2.0 * scaled_depth))
    return 0.5 * (1.0 + depth_ratio) * angular / wavenumber

def propagate_one(energy, frequency, water_depth, east_current, north_current, cosine_table, sine_table, wet_mask):
    celerity = celerity_one(frequency, water_depth)
    vel_x = celerity * cosine_table + east_current[:, None, :]
    vel_y = celerity * sine_table + north_current[:, None, :]
    plus_x = jnp.maximum(vel_x, 0.0) * energy
    minus_x = jnp.minimum(vel_x, 0.0) * energy
    plus_y = jnp.maximum(vel_y, 0.0) * energy
    minus_y = jnp.minimum(vel_y, 0.0) * energy
    diverge_x = plus_x + jnp.roll(minus_x, -1, axis=2) - jnp.roll(plus_x, 1, axis=2) - minus_x
    zero_row = jnp.zeros_like(plus_y[:1])
    diverge_y = plus_y + jnp.concatenate([minus_y[1:], zero_row], 0) - jnp.concatenate([zero_row, plus_y[:-1]], 0) - minus_y
    return (energy - COURANT * (diverge_x + diverge_y)) * wet_mask[:, None, :]

def relax_all(energy, frequency, dir_count):
    weight = BAND_WIDTH * (2.0 * math.pi / dir_count) * frequency

    def accumulate(carry, member):
        level = lax.optimization_barrier(jnp.sum(member[0], axis=1))
        return ((carry[0] + member[1] * level, carry[1] + member[1] * member[2] * level), None)
    start = jnp.zeros((energy.shape[1], energy.shape[3]), jnp.float32)
    totals, unused = lax.scan(accumulate, (start, start), (energy, weight, frequency))
    zeroth, first_moment = totals
    mean_freq = first_moment / jnp.maximum(zeroth, MOMENT_FLOOR)
    strength = DISSIPATION * zeroth * mean_freq

    def damp(member):
        return member[0] / (1.0 + strength[:, None, :] * (member[1] * member[1]))
    return lax.map(damp, (energy, frequency))

def reference(spectra, currents, bathymetry, sea_mask):
    wet_mask = sea_mask.astype(jnp.float32)
    row_count = spectra.shape[0]
    freq_count = spectra.shape[1]
    dir_count = spectra.shape[2]
    col_total = spectra.shape[3]
    per_set = col_total // N_PTS
    run_len = per_set // N_PTS
    grid = jnp.swapaxes(spectra.reshape(row_count, freq_count, dir_count, N_PTS, N_PTS, run_len), 3, 4).reshape(row_count, freq_count, dir_count, col_total)
    frequency = FREQ_FIRST * jnp.exp(jnp.arange(freq_count, dtype=jnp.int32).astype(jnp.float32) * math.log(FREQ_STEP))
    angles = jnp.arange(dir_count, dtype=jnp.float32) * (2.0 * math.pi / dir_count)
    cosine_table = jnp.cos(angles)[None, :, None]
    sine_table = jnp.sin(angles)[None, :, None]
    energy = jnp.moveaxis(grid, 1, 0) * wet_mask[None, :, None, :]
    for substep in range(currents.shape[0]):
        water_depth = bathymetry + currents[substep, 2]
        east_current = currents[substep, 0]
        north_current = currents[substep, 1]

        def advance(member):
            return propagate_one(member[0], member[1], water_depth, east_current, north_current, cosine_table, sine_table, wet_mask)
        energy = lax.map(advance, (energy, frequency))
        energy = relax_all(energy, frequency, dir_count)
    final_grid = jnp.moveaxis(energy, 0, 1)
    return jnp.swapaxes(final_grid.reshape(row_count, freq_count, dir_count, N_PTS, N_PTS, run_len), 3, 4).reshape(row_count, freq_count, dir_count, col_total)
```

```python
import math

import jax
import jax.numpy as jnp
from jax import lax
from jax.experimental import pallas as pl
from jax.experimental.pallas import tpu as pltpu
from jax.sharding import PartitionSpec as P

GRAVITY = 9.81
COURANT = 0.02
DISSIPATION = 1.0
MOMENT_FLOOR = 0.01
FREQ_FIRST = 0.035
FREQ_STEP = 1.1
BAND_WIDTH = 0.0955
ND = 36
NQ = 9
NFB = 9
ROWS = 16
BANDS = 4
PTS = 32
SUBSTEPS = 2
FIELDS = 8
LANES = 128
F32 = jnp.float32
VMEM_LIMIT = 40 * 1024 * 1024
VM = pl.BlockSpec(memory_space=pltpu.VMEM)
SM = pl.BlockSpec(memory_space=pltpu.SMEM)
PARAMS = pltpu.CompilerParams(vmem_limit_bytes=VMEM_LIMIT)


def lane_group():
    return lax.broadcasted_iota(jnp.int32, (ROWS, LANES), 1) & 3


def lroll(x, shift):
    return pltpu.roll(x, shift % LANES, 1)


def quad_transpose(a):
    lane = lane_group()
    low = lane < 2
    even = (lane & 1) == 0
    b0 = jnp.where(low, a[0], lroll(a[2], 2))
    b2 = jnp.where(low, lroll(a[0], -2), a[2])
    b1 = jnp.where(low, a[1], lroll(a[3], 2))
    b3 = jnp.where(low, lroll(a[1], -2), a[3])
    return (
        jnp.where(even, b0, lroll(b1, 1)),
        jnp.where(even, lroll(b0, -1), b1),
        jnp.where(even, b2, lroll(b3, 1)),
        jnp.where(even, lroll(b2, -1), b3),
    )


def quad_spread(x):
    lane = lane_group()
    low = lane < 2
    even = (lane & 1) == 0
    b0 = jnp.where(low, x, lroll(x, 2))
    b2 = jnp.where(low, lroll(x, -2), x)
    return (
        jnp.where(even, b0, lroll(b0, 1)),
        jnp.where(even, lroll(b0, -1), b0),
        jnp.where(even, b2, lroll(b2, 1)),
        jnp.where(even, lroll(b2, -1), b2),
    )


def quad_sum(x):
    lane = lane_group()
    x = x + jnp.where((lane & 1) == 0, lroll(x, -1), lroll(x, 1))
    return x + jnp.where(lane < 2, lroll(x, -2), lroll(x, 2))


def select4(x):
    lane = lane_group()
    return jnp.where(
        lane < 2, jnp.where(lane == 0, x[0], x[1]), jnp.where(lane == 2, x[2], x[3])
    )


def frequency_of(index):
    return FREQ_FIRST * jnp.exp(
        jnp.full((ROWS, LANES), index, jnp.int32).astype(F32) * math.log(FREQ_STEP)
    )


def edge_shifts(pts):
    left = jnp.where(pts == 0, 4, 0)
    right = jnp.where(pts == PTS - 1, LANES - 4, 0)
    return left, right


def pack_kernel(e_ref, ml_ref, mr_ref):
    for f in range(e_ref.shape[0]):
        for d in range(NQ):
            out = quad_transpose([e_ref[f, d + NQ * q] for q in range(4)])
            ml_ref[0, f, d] = out[0]
            ml_ref[1, f, d] = out[1]
            mr_ref[0, f, d] = out[2]
            mr_ref[1, f, d] = out[3]


def pack(spectra):
    fb = 3
    shape = jax.ShapeDtypeStruct((2, NFB, NQ, ROWS, LANES), F32)
    spec = pl.BlockSpec((2, fb, NQ, ROWS, LANES), lambda i: (0, i, 0, 0, 0))
    return pl.pallas_call(
        pack_kernel,
        grid=(NFB // fb,),
        in_specs=[pl.BlockSpec((fb, ND, ROWS, LANES), lambda i: (i, 0, 0, 0))],
        out_specs=[spec, spec],
        out_shape=[shape, shape],
        compiler_params=PARAMS,
        name="pack",
    )(spectra)


def exact_dot(a, b, dims):
    return lax.dot_general(
        a, b, (dims, ((), ())), precision=lax.Precision.HIGHEST, preferred_element_type=F32
    )


def forcing_kernel(at, f0, f1, f2, f3, out_ref, scr, full):
    band = at[0]
    for k, ref in enumerate((f0, f1, f2, f3)):
        scr[band ^ k] = ref[...]
    for q in range(BANDS):
        full[:, 4 * q : 4 * q + 4, :] = scr[q]
    shape = (8 * PTS, LANES)
    place = lax.broadcasted_iota(jnp.int32, shape, 0)
    wanted = (4 * (place >> 3) + (place & 7) + (LANES - 2)) & (LANES - 1)
    pick = (lax.broadcasted_iota(jnp.int32, shape, 1) == wanted).astype(F32)
    windows = exact_dot(pick, full[...].reshape(LANES, LANES), ((1,), (1,)))
    out_ref[...] = windows.reshape(PTS, 8, LANES)


def forcing_windows(at, parts):
    return pl.pallas_call(
        forcing_kernel,
        in_specs=[SM] + [VM] * 4,
        out_specs=VM,
        out_shape=jax.ShapeDtypeStruct((PTS, 8, LANES), F32),
        scratch_shapes=[
            pltpu.VMEM((BANDS, FIELDS, 4, LANES), F32),
            pltpu.VMEM((FIELDS, ROWS, LANES), F32),
        ],
        compiler_params=PARAMS,
        name="forcing",
    )(at, *parts)


def speed_kernel(at, win, c_ref, u_ref, v_ref, w_ref, t_ref, h_scr, f_scr):
    left, right = edge_shifts(at[1])
    shape = (PTS, LANES)
    place = lax.broadcasted_iota(jnp.int32, shape, 0)
    spread = ((lax.broadcasted_iota(jnp.int32, shape, 1) >> 2) == place).astype(F32)
    for i in range(8):
        fields = exact_dot(win[:, i, :], spread, ((0,), (0,)))
        if i < 2:
            fields = pltpu.roll(fields, left, 1)
        if i >= 6:
            fields = pltpu.roll(fields, right, 1)
        f_scr[i] = fields.reshape(FIELDS, ROWS, LANES)
    for i in range(8):
        w_ref[i] = f_scr[i, 7]
        for s in range(SUBSTEPS):
            u_ref[s, i] = COURANT * f_scr[i, 3 * s]
            v_ref[s, i] = COURANT * f_scr[i, 3 * s + 1]
    for s in range(SUBSTEPS):
        depth = [f_scr[i, 6] + f_scr[i, 3 * s + 2] for i in range(8)]
        h_scr[s, 0] = select4(depth[2:6])
        h_scr[s, 1] = select4([depth[6], depth[7], depth[0], depth[1]])

    def columns(x, y):
        a, b = quad_spread(x), quad_spread(y)
        return (b[2], b[3]) + a + (b[0], b[1])

    for d in range(NQ):
        angle = (d + NQ * lane_group()[0:8]).astype(F32) * (2.0 * math.pi / ND)
        t_ref[0, d] = jnp.cos(angle)
        t_ref[1, d] = jnp.sin(angle)
    first = at[0] * NFB

    def body(f, carry):
        angular = (2.0 * math.pi) * frequency_of(first + f)
        deep = angular * angular / GRAVITY
        for s in range(SUBSTEPS):
            speed = []
            for part in range(2):
                height = h_scr[s, part]
                wavenumber = deep / jnp.sqrt(jnp.tanh(deep * height))
                q = 2.0 * wavenumber * height
                ratio = 2.0 * q * jnp.exp(-q) / (1.0 - jnp.exp(-2.0 * q))
                speed.append((0.5 * COURANT) * (1.0 + ratio) * angular / wavenumber)
            for i, x in enumerate(columns(*speed)):
                c_ref[s, f, i] = x
        return carry

    lax.fori_loop(0, NFB, body, 0)


def speeds(at, windows):
    return pl.pallas_call(
        speed_kernel,
        in_specs=[SM, VM],
        out_specs=[VM] * 5,
        out_shape=[
            jax.ShapeDtypeStruct((SUBSTEPS, NFB, 8, ROWS, LANES), F32),
            jax.ShapeDtypeStruct((SUBSTEPS, 8, ROWS, LANES), F32),
            jax.ShapeDtypeStruct((SUBSTEPS, 8, ROWS, LANES), F32),
            jax.ShapeDtypeStruct((8, ROWS, LANES), F32),
            jax.ShapeDtypeStruct((2, NQ, 8, LANES), F32),
        ],
        scratch_shapes=[
            pltpu.VMEM((SUBSTEPS, 2, ROWS, LANES), F32),
            pltpu.VMEM((8, FIELDS, ROWS, LANES), F32),
        ],
        compiler_params=PARAMS,
        name="speeds",
    )(at, windows)


def row_below(x):
    first = lax.broadcasted_iota(jnp.int32, (8, LANES), 0) == 0
    t0, t1 = pltpu.roll(x[0:8], 1, 0), pltpu.roll(x[8:16], 1, 0)
    return jnp.concatenate([jnp.where(first, 0.0, t0), jnp.where(first, t0, t1)], axis=0)


def row_above(x):
    last = lax.broadcasted_iota(jnp.int32, (8, LANES), 0) == 7
    t0, t1 = pltpu.roll(x[0:8], 7, 0), pltpu.roll(x[8:16], 7, 0)
    return jnp.concatenate([jnp.where(last, t1, t0), jnp.where(last, 0.0, t1)], axis=0)


def advance(count, energy, speed, current_x, current_y, wet, cos, sin, store):
    inflow = None
    part = None
    for i in range(count):
        e = energy(i)
        c = speed(i)
        a = (c * cos + current_x(i)) * e
        if part is not None:
            store(i - 1, (part - jnp.minimum(a, 0.0)) * wet(i - 1))
        if 0 < i < count - 1:
            b = (c * sin + current_y(i)) * e
            turn = row_below(jnp.maximum(b, 0.0)) - row_above(jnp.minimum(b, 0.0))
            part = e - (jnp.abs(a) + jnp.abs(b)) + (inflow + turn)
        inflow = jnp.maximum(a, 0.0)


def twice(x):
    return jnp.concatenate([x, x], axis=0)


def add_moments(acc, levels, freq):
    weight = (BAND_WIDTH * (2.0 * math.pi / ND)) * freq
    for i, level in enumerate(levels):
        t = level * weight
        acc[0, i] = acc[0, i] + t
        acc[1, i] = acc[1, i] + t * freq


def first_kernel(at, lh, ml, mr, rh, c_ref, u_ref, v_ref, w_ref, t_ref, out_ref, mom_ref, acc):
    left, right = edge_shifts(at[1])
    first = at[0] * NFB
    acc[...] = jnp.zeros_like(acc)

    def body(f, carry):
        levels = [None] * 6
        for d in range(NQ):

            def energy(i):
                e = (lh, ml, mr, rh)[i // 2][i % 2, f, d]
                if i < 2:
                    e = pltpu.roll(e, left, 1)
                if i >= 6:
                    e = pltpu.roll(e, right, 1)
                return e * w_ref[i]

            def store(i, value):
                out_ref[i - 1, f, d] = value
                old = levels[i - 1]
                levels[i - 1] = value if old is None else old + value

            advance(
                8,
                energy,
                lambda i: c_ref[0, f, i],
                lambda i: u_ref[0, i],
                lambda i: v_ref[0, i],
                lambda i: w_ref[i],
                twice(t_ref[0, d]),
                twice(t_ref[1, d]),
                store,
            )
        add_moments(acc, levels, frequency_of(first + f))
        return carry

    lax.fori_loop(0, NFB, body, 0)
    for m in range(2):
        sums = [quad_sum(acc[m, i]) for i in range(6)]
        mom_ref[m, 0] = select4(sums[1:5])
        mom_ref[m, 1] = jnp.where(lane_group() < 2, sums[0], sums[5])


def first_step(at, lh, ml, mr, rh, c, u, v, w, t):
    return pl.pallas_call(
        first_kernel,
        in_specs=[SM] + [VM] * 9,
        out_specs=[VM] * 2,
        out_shape=[
            jax.ShapeDtypeStruct((6, NFB, NQ, ROWS, LANES), F32),
            jax.ShapeDtypeStruct((2, 2, ROWS, LANES), F32),
        ],
        scratch_shapes=[pltpu.VMEM((2, 6, ROWS, LANES), F32)],
        compiler_params=PARAMS,
        name="first_step",
    )(at, lh, ml, mr, rh, c, u, v, w, t)


def strength_of(parts, k):
    def total(m):
        a = [p[(m,) + k] for p in parts]
        return (a[0] + a[1]) + (a[2] + a[3])

    zeroth, first_moment = total(0), total(1)
    return DISSIPATION * zeroth * (first_moment / jnp.maximum(zeroth, MOMENT_FLOOR))


def second_kernel(
    at, e_ref, m0, m1, m2, m3, c_ref, u_ref, v_ref, w_ref, t_ref, out_ref, mom_ref, acc, s_scr, d_scr
):
    first = at[0] * NFB
    acc[...] = jnp.zeros_like(acc)
    own = quad_spread(strength_of((m0, m1, m2, m3), (0,)))
    edge = quad_spread(strength_of((m0, m1, m2, m3), (1,)))
    for i, x in enumerate((edge[0],) + own + (edge[2],)):
        s_scr[i] = x

    def body(f, carry):
        freq = frequency_of(first + f)
        square = freq * freq
        for i in range(6):
            d_scr[i] = 1.0 / (1.0 + s_scr[i] * square)
        levels = [None] * 4
        for d in range(NQ):

            def store(i, value):
                out_ref[i - 1, f, d] = value
                old = levels[i - 1]
                levels[i - 1] = value if old is None else old + value

            advance(
                6,
                lambda i: e_ref[i, f, d] * d_scr[i],
                lambda i: c_ref[1, f, i + 1],
                lambda i: u_ref[1, i + 1],
                lambda i: v_ref[1, i + 1],
                lambda i: w_ref[i + 1],
                twice(t_ref[0, d]),
                twice(t_ref[1, d]),
                store,
            )
        add_moments(acc, levels, freq)
        return carry

    lax.fori_loop(0, NFB, body, 0)
    for m in range(2):
        mom_ref[m] = select4([quad_sum(acc[m, i]) for i in range(4)])


def second_step(at, e, moments, c, u, v, w, t):
    return pl.pallas_call(
        second_kernel,
        in_specs=[SM] + [VM] * 10,
        out_specs=[VM] * 2,
        out_shape=[
            jax.ShapeDtypeStruct((4, NFB, NQ, ROWS, LANES), F32),
            jax.ShapeDtypeStruct((2, ROWS, LANES), F32),
        ],
        scratch_shapes=[
            pltpu.VMEM((2, 4, ROWS, LANES), F32),
            pltpu.VMEM((6, ROWS, LANES), F32),
            pltpu.VMEM((6, ROWS, LANES), F32),
        ],
        compiler_params=PARAMS,
        name="second_step",
    )(at, e, *moments, c, u, v, w, t)


def last_kernel(at, e_ref, m0, m1, m2, m3, out_ref):
    fb = e_ref.shape[1]
    first = at[0] * NFB + pl.program_id(0) * fb
    strength = strength_of((m0, m1, m2, m3), ())
    for f in range(fb):
        freq = frequency_of(first + f)
        damp = 1.0 / (1.0 + strength * (freq * freq))
        for d in range(NQ):
            out = quad_transpose([e_ref[c, f, d] for c in range(4)])
            for q in range(4):
                out_ref[f, d + NQ * q] = out[q] * damp


def last_step(at, e, moments):
    fb = 3
    small = pl.BlockSpec((2, ROWS, LANES), lambda i: (0, 0, 0))
    return pl.pallas_call(
        last_kernel,
        grid=(NFB // fb,),
        in_specs=[SM, pl.BlockSpec((4, fb, NQ, ROWS, LANES), lambda i: (0, i, 0, 0, 0))]
        + [small] * 4,
        out_specs=pl.BlockSpec((fb, ND, ROWS, LANES), lambda i: (i, 0, 0, 0)),
        out_shape=jax.ShapeDtypeStruct((NFB, ND, ROWS, LANES), F32),
        compiler_params=PARAMS,
        name="last_step",
    )(at, e, *moments)


RIGHT = [(i, (i + 1) % PTS) for i in range(PTS)]
LEFT = [(b, a) for a, b in RIGHT]


def band_parts(x):
    return [x] + [
        lax.ppermute(x, "band", [(i, i ^ k) for i in range(BANDS)]) for k in range(1, BANDS)
    ]


def per_device(spectra, currents, bathymetry, sea_mask):
    forcing = jnp.concatenate(
        [
            currents.reshape(3 * SUBSTEPS, 4, LANES),
            bathymetry[None],
            sea_mask.astype(F32)[None],
        ],
        0,
    )
    at = jnp.stack([lax.axis_index("band"), lax.axis_index("pts")]).astype(jnp.int32)
    ml, mr = pack(jnp.transpose(spectra, (1, 2, 0, 3)))
    lh = lax.ppermute(mr, "pts", RIGHT)
    rh = lax.ppermute(ml, "pts", LEFT)
    windows = forcing_windows(at, band_parts(forcing))
    windows = lax.all_to_all(windows, "pts", 0, 0, tiled=True)
    tables = speeds(at, windows)
    e, moments = first_step(at, lh, ml, mr, rh, *tables)
    e, moments = second_step(at, e, band_parts(moments), *tables)
    return jnp.transpose(last_step(at, e, band_parts(moments)), (2, 0, 1, 3))


def solution(mesh):
    in_specs = (
        P(None, "band", None, "pts"),
        P(None, None, "band", "pts"),
        P("band", "pts"),
        P("band", "pts"),
    )
    out_specs = P(None, "band", None, "pts")
    return jax.shard_map(
        per_device, mesh=mesh, in_specs=in_specs, out_specs=out_specs, check_vma=False
    )
```

```python
import math

import jax
import jax.numpy as jnp
from jax import lax
from jax.experimental import pallas as pl
from jax.experimental.pallas import tpu as pltpu
from jax.sharding import PartitionSpec as P

GRAVITY = 9.81
COURANT = 0.02
DISSIPATION = 1.0
MOMENT_FLOOR = 0.01
FREQ_FIRST = 0.035
FREQ_STEP = 1.1
BAND_WIDTH = 0.0955
ND = 36
NQ = 9
NFB = 9
ROWS = 16
BANDS = 4
PTS = 32
SUBSTEPS = 2
FIELDS = 8
LANES = 128
F32 = jnp.float32
VMEM_LIMIT = 40 * 1024 * 1024
VM = pl.BlockSpec(memory_space=pltpu.VMEM)
SM = pl.BlockSpec(memory_space=pltpu.SMEM)
HB = pl.BlockSpec(memory_space=pltpu.HBM)
PARAMS = pltpu.CompilerParams(vmem_limit_bytes=VMEM_LIMIT)


def lane_group():
    return lax.broadcasted_iota(jnp.int32, (ROWS, LANES), 1) & 3


def lroll(x, shift):
    return pltpu.roll(x, shift % LANES, 1)


def lane_swap(x, distance):
    index = lax.broadcasted_iota(jnp.int32, x.shape, 1) ^ distance
    return jnp.take_along_axis(x, index, axis=1)


def quad_transpose(a):
    lane = lane_group()

    def exchange(x, y, distance):
        low = (lane & distance) == 0
        t = lane_swap(jnp.where(low, y, x), distance)
        return jnp.where(low, x, t), jnp.where(low, t, y)

    b0, b2 = exchange(a[0], a[2], 2)
    b1, b3 = exchange(a[1], a[3], 2)
    o0, o1 = exchange(b0, b1, 1)
    o2, o3 = exchange(b2, b3, 1)
    return o0, o1, o2, o3


def quad_spread(x):
    lane = lax.broadcasted_iota(jnp.int32, x.shape, 1)
    return tuple(jnp.take_along_axis(x, (lane & ~3) + k, axis=1) for k in range(4))


def quad_sum(x):
    x = x + lane_swap(x, 1)
    return x + lane_swap(x, 2)


def select4(x):
    lane = lane_group()
    return jnp.where(
        lane < 2, jnp.where(lane == 0, x[0], x[1]), jnp.where(lane == 2, x[2], x[3])
    )


def frequency_of(index):
    return FREQ_FIRST * jnp.exp(
        jnp.full((ROWS, LANES), index, jnp.int32).astype(F32) * math.log(FREQ_STEP)
    )


def edge_shifts(pts):
    left = jnp.where(pts == 0, 4, 0)
    right = jnp.where(pts == PTS - 1, LANES - 4, 0)
    return left, right


def cost(microseconds):
    return pl.CostEstimate(
        flops=0, transcendentals=0, bytes_accessed=int(microseconds * 3.0e6)
    )


def loop(count, body):
    lax.fori_loop(0, count, lambda i, carry: (body(i), carry)[1], 0)


def pack_kernel(e_ref, ml_ref, mr_ref):
    def body(f):
        def over(d, carry):
            out = quad_transpose([e_ref[f, d + NQ * q] for q in range(4)])
            ml_ref[0, f, d] = out[0]
            ml_ref[1, f, d] = out[1]
            mr_ref[0, f, d] = out[2]
            mr_ref[1, f, d] = out[3]
            return carry

        lax.fori_loop(0, NQ, over, 0, unroll=3)

    loop(NFB, body)


def pack(spectra):
    shape = jax.ShapeDtypeStruct((2, NFB, NQ, ROWS, LANES), F32)
    return pl.pallas_call(
        pack_kernel,
        in_specs=[VM],
        out_specs=[VM, VM],
        out_shape=[shape, shape],
        compiler_params=PARAMS,
        cost_estimate=cost(2.0),
        name="pack",
    )(spectra)


def exact_dot(a, b, dims):
    return lax.dot_general(
        a, b, (dims, ((), ())), precision=lax.Precision.HIGHEST, preferred_element_type=F32
    )


def forcing_kernel(own, out_ref):
    shape = (8 * PTS, LANES)
    place = lax.broadcasted_iota(jnp.int32, shape, 0)
    wanted = (4 * (place & (PTS - 1)) + (place >> 5) + (LANES - 2)) & (LANES - 1)
    pick = (lax.broadcasted_iota(jnp.int32, shape, 1) == wanted).astype(F32)
    x = exact_dot(pick, own[...], ((1,), (1,)))
    for h in range(2):
        row = jnp.concatenate(
            [x[PTS * (4 * h + k) : PTS * (4 * h + k) + PTS] for k in range(4)], axis=1
        )
        for band in range(BANDS):
            out_ref[PTS * band : PTS * band + PTS, h, :] = row


def forcing_windows(forcing):
    return pl.pallas_call(
        forcing_kernel,
        in_specs=[VM],
        out_specs=VM,
        out_shape=jax.ShapeDtypeStruct((BANDS * PTS, 2, LANES), F32),
        compiler_params=PARAMS,
        cost_estimate=cost(0.8),
        name="forcing",
    )(forcing)


def spread_columns(x, y):
    a, b = quad_spread(x), quad_spread(y)
    return (b[2], b[3]) + a + (b[0], b[1])


def celerities(first, h_ref, c_ref):
    def body(f):
        angular = (2.0 * math.pi) * frequency_of(first + f)
        deep = angular * angular / GRAVITY
        speed = []
        for part in range(2):
            height = h_ref[part]
            wavenumber = deep / jnp.sqrt(jnp.tanh(deep * height))
            q = 2.0 * wavenumber * height
            ratio = 2.0 * q * jnp.exp(-q) / (1.0 - jnp.exp(-2.0 * q))
            speed.append((0.5 * COURANT) * (1.0 + ratio) * angular / wavenumber)
        for i, x in enumerate(spread_columns(*speed)):
            c_ref[f, i] = x

    loop(NFB, body)


def speed_kernel(at, win, c_ref, u_ref, v_ref, w_ref, t_ref, h_ref, f_scr, h_scr):
    left, right = edge_shifts(at[1])
    shape = (PTS, LANES)
    place = lax.broadcasted_iota(jnp.int32, shape, 0)
    spread = ((lax.broadcasted_iota(jnp.int32, shape, 1) >> 2) == place).astype(F32)
    for band in range(BANDS):
        for h in range(2):
            block = win[PTS * band : PTS * band + PTS, h, :]
            fields = exact_dot(block, spread, ((0,), (0,)))
            for k in range(4):
                i = 4 * h + k
                part = fields[32 * k : 32 * k + 32]
                if i < 2:
                    part = pltpu.roll(part, left, 1)
                if i >= 6:
                    part = pltpu.roll(part, right, 1)
                for n in range(FIELDS):
                    f_scr[i, n, 4 * band : 4 * band + 4, :] = part[4 * n : 4 * n + 4]
    for i in range(8):
        w_ref[i] = f_scr[i, 7]
        for s in range(SUBSTEPS):
            u_ref[s, i] = COURANT * f_scr[i, 3 * s]
            v_ref[s, i] = COURANT * f_scr[i, 3 * s + 1]
    for s, ref in ((0, h_scr), (1, h_ref)):
        depth = [f_scr[i, 6] + f_scr[i, 3 * s + 2] for i in range(8)]
        ref[0] = select4(depth[2:6])
        ref[1] = select4([depth[6], depth[7], depth[0], depth[1]])
    for d in range(NQ):
        angle = (d + NQ * lane_group()[0:8]).astype(F32) * (2.0 * math.pi / ND)
        t_ref[0, d] = jnp.cos(angle)
        t_ref[1, d] = jnp.sin(angle)
    celerities(at[0] * NFB, h_scr, c_ref)


def speeds(at, windows):
    return pl.pallas_call(
        speed_kernel,
        in_specs=[SM, VM],
        out_specs=[VM] * 6,
        out_shape=[
            jax.ShapeDtypeStruct((NFB, 8, ROWS, LANES), F32),
            jax.ShapeDtypeStruct((SUBSTEPS, 8, ROWS, LANES), F32),
            jax.ShapeDtypeStruct((SUBSTEPS, 8, ROWS, LANES), F32),
            jax.ShapeDtypeStruct((8, ROWS, LANES), F32),
            jax.ShapeDtypeStruct((2, NQ, 8, LANES), F32),
            jax.ShapeDtypeStruct((2, ROWS, LANES), F32),
        ],
        scratch_shapes=[
            pltpu.VMEM((8, FIELDS, ROWS, LANES), F32),
            pltpu.VMEM((2, ROWS, LANES), F32),
        ],
        compiler_params=PARAMS,
        cost_estimate=cost(2.0),
        name="speeds",
    )(at, windows)


def second_speed_kernel(at, h_ref, c_ref):
    celerities(at[0] * NFB, h_ref, c_ref)


def second_speeds(at, h):
    return pl.pallas_call(
        second_speed_kernel,
        in_specs=[SM, VM],
        out_specs=VM,
        out_shape=jax.ShapeDtypeStruct((NFB, 8, ROWS, LANES), F32),
        compiler_params=PARAMS,
        cost_estimate=cost(1.5),
        name="second_speeds",
    )(at, h)


def row_below(x):
    first = lax.broadcasted_iota(jnp.int32, (8, LANES), 0) == 0
    t0, t1 = pltpu.roll(x[0:8], 1, 0), pltpu.roll(x[8:16], 1, 0)
    return jnp.concatenate([jnp.where(first, 0.0, t0), jnp.where(first, t0, t1)], axis=0)


def row_above(x):
    last = lax.broadcasted_iota(jnp.int32, (8, LANES), 0) == 7
    t0, t1 = pltpu.roll(x[0:8], 7, 0), pltpu.roll(x[8:16], 7, 0)
    return jnp.concatenate([jnp.where(last, t1, t0), jnp.where(last, 0.0, t1)], axis=0)


def advance(count, energy, speed, current_x, current_y, wet, cos, sin, store):
    inflow = None
    part = None
    for i in range(count):
        e = energy(i)
        c = speed(i)
        a = (c * cos + current_x(i)) * e
        if part is not None:
            store(i - 1, (part - jnp.minimum(a, 0.0)) * wet(i - 1))
        if 0 < i < count - 1:
            b = (c * sin + current_y(i)) * e
            turn = row_below(jnp.maximum(b, 0.0)) - row_above(jnp.minimum(b, 0.0))
            part = e - (jnp.abs(a) + jnp.abs(b)) + (inflow + turn)
        inflow = jnp.maximum(a, 0.0)


UNROLL = 9


def zeros(count):
    return tuple(jnp.zeros((ROWS, LANES), F32) for _ in range(count))


def twice(x):
    return jnp.concatenate([x, x], axis=0)


def add_moments(acc, levels, freq):
    weight = (BAND_WIDTH * (2.0 * math.pi / ND)) * freq
    for i, level in enumerate(levels):
        t = level * weight
        acc[0, i] = acc[0, i] + t
        acc[1, i] = acc[1, i] + t * freq


def inner_kernel(
    at, ml, mr, c_ref, u_ref, v_ref, w_ref, t_ref, out_ref, left_ref, right_ref, acc_ref
):
    first = at[0] * NFB
    acc_ref[...] = jnp.zeros_like(acc_ref)

    def body(f, carry):
        def over(d, levels):
            levels = list(levels)
            cos, sin = twice(t_ref[0, d]), twice(t_ref[1, d])
            inflow = None
            part = None
            for i in range(4):
                e = (ml, mr)[i // 2][i % 2, f, d] * w_ref[i + 2]
                c = c_ref[f, i + 2]
                a = (c * cos + u_ref[0, i + 2]) * e
                minus = jnp.minimum(a, 0.0)
                if i == 0:
                    left_ref[f, d] = minus
                if i == 1:
                    out_ref[0, f, d] = part - minus
                if i > 1:
                    value = (part - minus) * w_ref[i + 1]
                    out_ref[i - 1, f, d] = value
                    levels[i - 2] = levels[i - 2] + value
                b = (c * sin + v_ref[0, i + 2]) * e
                turn = row_below(jnp.maximum(b, 0.0)) - row_above(jnp.minimum(b, 0.0))
                part = e - (jnp.abs(a) + jnp.abs(b))
                part = part + (turn if inflow is None else inflow + turn)
                inflow = jnp.maximum(a, 0.0)
            out_ref[3, f, d] = part
            right_ref[f, d] = inflow
            return tuple(levels)

        levels = lax.fori_loop(0, NQ, over, zeros(2), unroll=UNROLL)
        add_moments(acc_ref, levels, frequency_of(first + f))
        return carry

    lax.fori_loop(0, NFB, body, 0)


def inner_step(at, ml, mr, c, u, v, w, t):
    edge = jax.ShapeDtypeStruct((NFB, NQ, ROWS, LANES), F32)
    return pl.pallas_call(
        inner_kernel,
        in_specs=[SM] + [VM] * 7,
        out_specs=[VM] * 4,
        out_shape=[
            jax.ShapeDtypeStruct((4, NFB, NQ, ROWS, LANES), F32),
            edge,
            edge,
            jax.ShapeDtypeStruct((2, 2, ROWS, LANES), F32),
        ],
        compiler_params=PARAMS,
        cost_estimate=cost(4.0),
        name="inner_step",
    )(at, ml, mr, c, u, v, w, t)


def outer_kernel(
    at, lh, rh, e_ref, l_ref, r_ref, a_ref, c_ref, u_ref, v_ref, w_ref, t_ref, out_ref, mom_ref, acc
):
    left, right = edge_shifts(at[1])
    first = at[0] * NFB
    acc[...] = jnp.zeros_like(acc)

    def body(f, carry):
        def over(d, levels):
            levels = list(levels)
            cos, sin = twice(t_ref[0, d]), twice(t_ref[1, d])

            def load(i):
                if i < 2:
                    e = pltpu.roll(lh[i, f, d], left, 1)
                else:
                    e = pltpu.roll(rh[i - 6, f, d], right, 1)
                e = e * w_ref[i]
                return e, (c_ref[f, i] * cos + u_ref[0, i]) * e

            def stay(i, e, a):
                b = (c_ref[f, i] * sin + v_ref[0, i]) * e
                turn = row_below(jnp.maximum(b, 0.0)) - row_above(jnp.minimum(b, 0.0))
                return e - (jnp.abs(a) + jnp.abs(b)) + turn

            def store(k, i, value):
                value = value * w_ref[i]
                out_ref[k, f, d] = value
                levels[k] = levels[k] + value

            _, a0 = load(0)
            e1, a1 = load(1)
            store(0, 1, stay(1, e1, a1) + jnp.maximum(a0, 0.0) - l_ref[f, d])
            store(1, 2, e_ref[0, f, d] + jnp.maximum(a1, 0.0))
            e6, a6 = load(6)
            _, a7 = load(7)
            store(2, 5, e_ref[3, f, d] - jnp.minimum(a6, 0.0))
            store(3, 6, stay(6, e6, a6) + r_ref[f, d] - jnp.minimum(a7, 0.0))
            return tuple(levels)

        levels = lax.fori_loop(0, NQ, over, zeros(4), unroll=UNROLL)
        add_moments(acc, levels, frequency_of(first + f))
        return carry

    lax.fori_loop(0, NFB, body, 0)
    for m in range(2):
        parts = [acc[m, 1], a_ref[m, 0], a_ref[m, 1], acc[m, 2]]
        mom_ref[m, 0] = select4([quad_sum(x) for x in parts])
        mom_ref[m, 1] = jnp.where(lane_group() < 2, quad_sum(acc[m, 0]), quad_sum(acc[m, 3]))


def outer_step(at, lh, rh, inner, tables):
    return pl.pallas_call(
        outer_kernel,
        in_specs=[SM] + [VM] * 11,
        out_specs=[VM] * 2,
        out_shape=[
            jax.ShapeDtypeStruct((4, NFB, NQ, ROWS, LANES), F32),
            jax.ShapeDtypeStruct((2, 2, ROWS, LANES), F32),
        ],
        scratch_shapes=[pltpu.VMEM((2, 4, ROWS, LANES), F32)],
        compiler_params=PARAMS,
        cost_estimate=cost(3.0),
        name="outer_step",
    )(at, lh, rh, *inner, *tables)


def strength_of(parts, k):
    def total(m):
        a = [p[(m,) + k] for p in parts]
        return (a[0] + a[1]) + (a[2] + a[3])

    zeroth, first_moment = total(0), total(1)
    return DISSIPATION * zeroth * (first_moment / jnp.maximum(zeroth, MOMENT_FLOOR))


def second_kernel(
    at, in_ref, edge_ref, m0, m1, m2, m3, c_ref, u_ref, v_ref, w_ref, t_ref,
    out_ref, mom_ref, acc, s_scr, d_scr,
):
    first = at[0] * NFB
    acc[...] = jnp.zeros_like(acc)
    own = quad_spread(strength_of((m0, m1, m2, m3), (0,)))
    edge = quad_spread(strength_of((m0, m1, m2, m3), (1,)))
    for i, x in enumerate((edge[0],) + own + (edge[2],)):
        s_scr[i] = x

    def body(f, carry):
        freq = frequency_of(first + f)
        square = freq * freq
        for i in range(6):
            d_scr[i] = 1.0 / (1.0 + s_scr[i] * square)
        def over(d, levels):
            levels = list(levels)

            def store(i, value):
                out_ref[i - 1, f, d] = value
                levels[i - 1] = levels[i - 1] + value

            def energy(i):
                if i in (2, 3):
                    return in_ref[i - 1, f, d] * d_scr[i]
                return edge_ref[(0, 1, 0, 0, 2, 3)[i], f, d] * d_scr[i]

            advance(
                6,
                energy,
                lambda i: c_ref[f, i + 1],
                lambda i: u_ref[1, i + 1],
                lambda i: v_ref[1, i + 1],
                lambda i: w_ref[i + 1],
                twice(t_ref[0, d]),
                twice(t_ref[1, d]),
                store,
            )
            return tuple(levels)

        levels = lax.fori_loop(0, NQ, over, zeros(4), unroll=UNROLL)
        add_moments(acc, levels, freq)
        return carry

    lax.fori_loop(0, NFB, body, 0)
    for m in range(2):
        mom_ref[m] = select4([quad_sum(acc[m, i]) for i in range(4)])


def second_step(at, e, edges, moments, c, u, v, w, t):
    return pl.pallas_call(
        second_kernel,
        in_specs=[SM] + [VM] * 11,
        out_specs=[VM] * 2,
        out_shape=[
            jax.ShapeDtypeStruct((4, NFB, NQ, ROWS, LANES), F32),
            jax.ShapeDtypeStruct((2, ROWS, LANES), F32),
        ],
        scratch_shapes=[
            pltpu.VMEM((2, 4, ROWS, LANES), F32),
            pltpu.VMEM((6, ROWS, LANES), F32),
            pltpu.VMEM((6, ROWS, LANES), F32),
        ],
        compiler_params=PARAMS,
        cost_estimate=cost(3.5),
        name="second_step",
    )(at, e, edges, *moments, c, u, v, w, t)


def unpack_kernel(e_ref, out_ref):
    def body(f, carry):
        for d in range(NQ):
            out = quad_transpose([e_ref[c, f, d] for c in range(4)])
            for q in range(4):
                out_ref[f, d + NQ * q] = out[q]
        return carry

    lax.fori_loop(0, NFB, body, 0)


def unpack(e):
    return pl.pallas_call(
        unpack_kernel,
        in_specs=[VM],
        out_specs=VM,
        out_shape=jax.ShapeDtypeStruct((NFB, ND, ROWS, LANES), F32),
        compiler_params=PARAMS,
        cost_estimate=cost(2.0),
        name="unpack",
    )(e)


def last_kernel(at, e_ref, m0, m1, m2, m3, out_hbm, buf, sem):
    first = at[0] * NFB
    strength = strength_of((m0, m1, m2, m3), ())

    def save(f):
        return pltpu.make_async_copy(buf.at[f], out_hbm.at[f], sem.at[f])

    def body(f, carry):
        freq = frequency_of(first + f)
        damp = 1.0 / (1.0 + strength * (freq * freq))
        for d in range(ND):
            buf[f, d] = e_ref[f, d] * damp
        save(f).start()
        return carry

    lax.fori_loop(0, NFB, body, 0)
    for f in range(NFB):
        save(f).wait()


def last_step(at, e, moments):
    return pl.pallas_call(
        last_kernel,
        in_specs=[SM] + [VM] * 5,
        out_specs=HB,
        out_shape=jax.ShapeDtypeStruct((NFB, ND, ROWS, LANES), F32),
        scratch_shapes=[
            pltpu.VMEM((NFB, ND, ROWS, LANES), F32),
            pltpu.SemaphoreType.DMA((NFB,)),
        ],
        compiler_params=PARAMS,
        cost_estimate=cost(1.5),
        name="last_step",
    )(at, e, *moments)


RIGHT = [(i, (i + 1) % PTS) for i in range(PTS)]
LEFT = [(b, a) for a, b in RIGHT]


def band_parts(x):
    return [x] + [
        lax.ppermute(x, "band", [(i, i ^ k) for i in range(BANDS)]) for k in range(1, BANDS)
    ]


def per_device(spectra, currents, bathymetry, sea_mask):
    forcing = jnp.concatenate(
        [
            currents.reshape(3 * SUBSTEPS, 4, LANES),
            bathymetry[None],
            sea_mask.astype(F32)[None],
        ],
        0,
    ).reshape(4 * FIELDS, LANES)
    at = jnp.stack([lax.axis_index("band"), lax.axis_index("pts")]).astype(jnp.int32)
    windows = forcing_windows(forcing)
    windows = lax.all_to_all(windows, ("band", "pts"), 0, 0, tiled=True)
    ml, mr = pack(jnp.transpose(spectra, (1, 2, 0, 3)))
    lh = lax.ppermute(mr, "pts", RIGHT)
    rh = lax.ppermute(ml, "pts", LEFT)
    *tables, depth = speeds(at, windows)
    inner = inner_step(at, ml, mr, *tables)
    edges, moments = outer_step(at, lh, rh, inner, tables)
    tables[0] = second_speeds(at, depth)
    e, moments = second_step(at, inner[0], edges, band_parts(moments), *tables)
    return jnp.transpose(last_step(at, unpack(e), band_parts(moments)), (2, 0, 1, 3))


def solution(mesh):
    in_specs = (
        P(None, "band", None, "pts"),
        P(None, None, "band", "pts"),
        P("band", "pts"),
        P("band", "pts"),
    )
    out_specs = P(None, "band", None, "pts")
    return jax.shard_map(
        per_device, mesh=mesh, in_specs=in_specs, out_specs=out_specs, check_vma=False
    )
```

```python
import math

import jax
import jax.numpy as jnp
from jax import lax
from jax.experimental import pallas as pl
from jax.experimental.pallas import tpu as pltpu
from jax.sharding import PartitionSpec as P

GRAVITY = 9.81
COURANT = 0.02
DISSIPATION = 1.0
MOMENT_FLOOR = 0.01
FREQ_FIRST = 0.035
FREQ_STEP = 1.1
BAND_WIDTH = 0.0955
ND = 36
NQ = 9
NFB = 9
ROWS = 16
BANDS = 4
PTS = 32
SUBSTEPS = 2
FIELDS = 8
LANES = 128
F32 = jnp.float32
VMEM_LIMIT = 40 * 1024 * 1024
VM = pl.BlockSpec(memory_space=pltpu.VMEM)
SM = pl.BlockSpec(memory_space=pltpu.SMEM)
HB = pl.BlockSpec(memory_space=pltpu.HBM)
PARAMS = pltpu.CompilerParams(vmem_limit_bytes=VMEM_LIMIT)


def lane_group():
    return lax.broadcasted_iota(jnp.int32, (ROWS, LANES), 1) & 3


def lroll(x, shift):
    return pltpu.roll(x, shift % LANES, 1)


def lane_swap(x, distance):
    index = lax.broadcasted_iota(jnp.int32, x.shape, 1) ^ distance
    return jnp.take_along_axis(x, index, axis=1)


def quad_transpose(a):
    lane = lane_group()

    def exchange(x, y, distance):
        low = (lane & distance) == 0
        t = lane_swap(jnp.where(low, y, x), distance)
        return jnp.where(low, x, t), jnp.where(low, t, y)

    b0, b2 = exchange(a[0], a[2], 2)
    b1, b3 = exchange(a[1], a[3], 2)
    o0, o1 = exchange(b0, b1, 1)
    o2, o3 = exchange(b2, b3, 1)
    return o0, o1, o2, o3


def quad_spread(x):
    lane = lax.broadcasted_iota(jnp.int32, x.shape, 1)
    return tuple(jnp.take_along_axis(x, (lane & ~3) + k, axis=1) for k in range(4))


def quad_sum(x):
    x = x + lane_swap(x, 1)
    return x + lane_swap(x, 2)


def select4(x):
    lane = lane_group()
    return jnp.where(
        lane < 2, jnp.where(lane == 0, x[0], x[1]), jnp.where(lane == 2, x[2], x[3])
    )


def frequency_of(index):
    return FREQ_FIRST * jnp.exp(
        jnp.full((ROWS, LANES), index, jnp.int32).astype(F32) * math.log(FREQ_STEP)
    )


def edge_shifts(pts):
    left = jnp.where(pts == 0, 4, 0)
    right = jnp.where(pts == PTS - 1, LANES - 4, 0)
    return left, right


def cost(microseconds):
    return pl.CostEstimate(
        flops=0, transcendentals=0, bytes_accessed=int(microseconds * 3.0e6)
    )


def loop(count, body):
    lax.fori_loop(0, count, lambda i, carry: (body(i), carry)[1], 0)


def load_rows(ref, lead):
    return jnp.concatenate(
        [ref[lead + (pl.ds(parity, 8, stride=2), slice(None))] for parity in range(2)], axis=0
    )


def store_rows(ref, lead, value):
    for parity in range(2):
        ref[lead + (pl.ds(parity, 8, stride=2), slice(None))] = value[8 * parity : 8 * parity + 8]


def pack_kernel(e_ref, ml_ref, mr_ref):
    def body(f):
        for d in range(NQ):
            out = quad_transpose([load_rows(e_ref, (f, d + NQ * q)) for q in range(4)])
            ml_ref[0, f, d] = out[0]
            ml_ref[1, f, d] = out[1]
            mr_ref[0, f, d] = out[2]
            mr_ref[1, f, d] = out[3]

    loop(NFB, body)


def pack(spectra):
    shape = jax.ShapeDtypeStruct((2, NFB, NQ, ROWS, LANES), F32)
    return pl.pallas_call(
        pack_kernel,
        in_specs=[VM],
        out_specs=[VM, VM],
        out_shape=[shape, shape],
        compiler_params=PARAMS,
        cost_estimate=cost(2.0),
        name="pack",
    )(spectra)


def exact_dot(a, b, dims):
    return lax.dot_general(
        a, b, (dims, ((), ())), precision=lax.Precision.HIGHEST, preferred_element_type=F32
    )


def forcing_kernel(own, out_ref):
    shape = (8 * PTS, LANES)
    place = lax.broadcasted_iota(jnp.int32, shape, 0)
    wanted = (4 * (place & (PTS - 1)) + (place >> 5) + (LANES - 2)) & (LANES - 1)
    pick = (lax.broadcasted_iota(jnp.int32, shape, 1) == wanted).astype(F32)
    x = exact_dot(pick, own[...], ((1,), (1,)))
    for h in range(2):
        row = jnp.concatenate(
            [x[PTS * (4 * h + k) : PTS * (4 * h + k) + PTS] for k in range(4)], axis=1
        )
        for band in range(BANDS):
            out_ref[PTS * band : PTS * band + PTS, h, :] = row


def forcing_windows(forcing):
    return pl.pallas_call(
        forcing_kernel,
        in_specs=[VM],
        out_specs=VM,
        out_shape=jax.ShapeDtypeStruct((BANDS * PTS, 2, LANES), F32),
        compiler_params=PARAMS,
        cost_estimate=cost(0.8),
        name="forcing",
    )(forcing)


def spread_columns(x, y):
    a, b = quad_spread(x), quad_spread(y)
    return (b[2], b[3]) + a + (b[0], b[1])


def celerities(first, h_ref, c_ref):
    def body(f):
        angular = (2.0 * math.pi) * frequency_of(first + f)
        deep = angular * angular / GRAVITY
        speed = []
        for part in range(2):
            height = h_ref[part]
            wavenumber = deep / jnp.sqrt(jnp.tanh(deep * height))
            q = 2.0 * wavenumber * height
            ratio = 2.0 * q * jnp.exp(-q) / (1.0 - jnp.exp(-2.0 * q))
            speed.append((0.5 * COURANT) * (1.0 + ratio) * angular / wavenumber)
        for i, x in enumerate(spread_columns(*speed)):
            c_ref[f, i] = x

    loop(NFB, body)


def speed_kernel(at, win, c_ref, u_ref, v_ref, w_ref, h_ref, f_scr, h_scr):
    left, right = edge_shifts(at[1])
    shape = (PTS, LANES)
    place = lax.broadcasted_iota(jnp.int32, shape, 0)
    spread = ((lax.broadcasted_iota(jnp.int32, shape, 1) >> 2) == place).astype(F32)
    for band in range(BANDS):
        for h in range(2):
            block = win[PTS * band : PTS * band + PTS, h, :]
            fields = exact_dot(block, spread, ((0,), (0,)))
            for k in range(4):
                i = 4 * h + k
                part = fields[32 * k : 32 * k + 32]
                if i < 2:
                    part = pltpu.roll(part, left, 1)
                if i >= 6:
                    part = pltpu.roll(part, right, 1)
                for n in range(FIELDS):
                    f_scr[i, n, 4 * band : 4 * band + 4, :] = part[4 * n : 4 * n + 4]
    for i in range(8):
        w_ref[i] = load_rows(f_scr, (i, 7))
        for s in range(SUBSTEPS):
            u_ref[s, i] = COURANT * load_rows(f_scr, (i, 3 * s))
            v_ref[s, i] = COURANT * load_rows(f_scr, (i, 3 * s + 1))
    for s, ref in ((0, h_scr), (1, h_ref)):
        depth = [load_rows(f_scr, (i, 6)) + load_rows(f_scr, (i, 3 * s + 2)) for i in range(8)]
        ref[0] = select4(depth[2:6])
        ref[1] = select4([depth[6], depth[7], depth[0], depth[1]])
    celerities(at[0] * NFB, h_scr, c_ref)


def speeds(at, windows):
    return pl.pallas_call(
        speed_kernel,
        in_specs=[SM, VM],
        out_specs=[VM] * 5,
        out_shape=[
            jax.ShapeDtypeStruct((NFB, 8, ROWS, LANES), F32),
            jax.ShapeDtypeStruct((SUBSTEPS, 8, ROWS, LANES), F32),
            jax.ShapeDtypeStruct((SUBSTEPS, 8, ROWS, LANES), F32),
            jax.ShapeDtypeStruct((8, ROWS, LANES), F32),
            jax.ShapeDtypeStruct((2, ROWS, LANES), F32),
        ],
        scratch_shapes=[
            pltpu.VMEM((8, FIELDS, ROWS, LANES), F32),
            pltpu.VMEM((2, ROWS, LANES), F32),
        ],
        compiler_params=PARAMS,
        cost_estimate=cost(2.0),
        name="speeds",
    )(at, windows)


def turn_kernel(t_ref):
    for d in range(NQ):
        angle = (d + NQ * lane_group()[0:8]).astype(F32) * (2.0 * math.pi / ND)
        t_ref[0, d] = jnp.cos(angle)
        t_ref[1, d] = jnp.sin(angle)


def turns():
    return pl.pallas_call(
        turn_kernel,
        out_specs=VM,
        out_shape=jax.ShapeDtypeStruct((2, NQ, 8, LANES), F32),
        compiler_params=PARAMS,
        cost_estimate=cost(0.5),
        name="turns",
    )()


def second_speed_kernel(at, h_ref, c_ref):
    celerities(at[0] * NFB, h_ref, c_ref)


def second_speeds(at, h):
    return pl.pallas_call(
        second_speed_kernel,
        in_specs=[SM, VM],
        out_specs=VM,
        out_shape=jax.ShapeDtypeStruct((NFB, 8, ROWS, LANES), F32),
        compiler_params=PARAMS,
        cost_estimate=cost(1.5),
        name="second_speeds",
    )(at, h)


def row_flux(b):
    sub = lax.broadcasted_iota(jnp.int32, (8, LANES), 0)
    plus, minus = jnp.maximum(b, 0.0), jnp.minimum(b, 0.0)
    even = plus[0:8] + minus[8:16]
    odd = plus[8:16] + jnp.where(sub == 7, 0.0, pltpu.roll(minus[0:8], 7, 0))
    before = jnp.where(sub == 0, minus[0:8], pltpu.roll(odd, 1, 0))
    return jnp.concatenate([even - before, odd - even], axis=0)


def advance(count, energy, speed, current_x, current_y, cos, sin, store):
    plus = None
    entered = None
    part = None
    for i in range(count):
        e = energy(i)
        c = speed(i)
        a = (c * cos + current_x(i)) * e
        if plus is not None:
            crossed = plus + jnp.minimum(a, 0.0)
            if part is not None:
                store(i - 1, part - crossed)
            entered = crossed
        if 0 < i < count - 1:
            b = (c * sin + current_y(i)) * e
            part = e + entered - row_flux(b)
        plus = jnp.maximum(a, 0.0)


UNROLL = 9


def zeros(count):
    return tuple(jnp.zeros((ROWS, LANES), F32) for _ in range(count))


def twice(x):
    return jnp.concatenate([x, x], axis=0)


def add_moments(acc, levels, wet, freq):
    weight = (BAND_WIDTH * (2.0 * math.pi / ND)) * freq
    for i, level in enumerate(levels):
        t = level * wet(i) * weight
        acc[0, i] = acc[0, i] + t
        acc[1, i] = acc[1, i] + t * freq


def first_kernel(at, lh, ml, mr, rh, c_ref, u_ref, v_ref, w_ref, t_ref, out_ref, mom_ref, acc):
    left, right = edge_shifts(at[1])
    first = at[0] * NFB
    acc[...] = jnp.zeros_like(acc)

    def body(f):
        def over(d, levels):
            levels = list(levels)

            def store(i, value):
                out_ref[i - 1, f, d] = value
                levels[i - 1] = levels[i - 1] + value

            def energy(i):
                e = (lh, ml, mr, rh)[i // 2][i % 2, f, d]
                if i < 2:
                    e = pltpu.roll(e, left, 1)
                if i >= 6:
                    e = pltpu.roll(e, right, 1)
                return e * w_ref[i]

            advance(
                8,
                energy,
                lambda i: c_ref[f, i],
                lambda i: u_ref[0, i],
                lambda i: v_ref[0, i],
                twice(t_ref[0, d]),
                twice(t_ref[1, d]),
                store,
            )
            return tuple(levels)

        levels = lax.fori_loop(0, NQ, over, zeros(6), unroll=UNROLL)
        add_moments(acc, levels, lambda i: w_ref[i + 1], frequency_of(first + f))

    loop(NFB, body)
    for m in range(2):
        sums = [quad_sum(acc[m, i]) for i in range(6)]
        mom_ref[m, 0] = select4(sums[1:5])
        mom_ref[m, 1] = jnp.where(lane_group() < 2, sums[0], sums[5])


def first_step(at, lh, ml, mr, rh, tables):
    return pl.pallas_call(
        first_kernel,
        in_specs=[SM] + [VM] * 9,
        out_specs=[VM] * 2,
        out_shape=[
            jax.ShapeDtypeStruct((6, NFB, NQ, ROWS, LANES), F32),
            jax.ShapeDtypeStruct((2, 2, ROWS, LANES), F32),
        ],
        scratch_shapes=[pltpu.VMEM((2, 6, ROWS, LANES), F32)],
        compiler_params=PARAMS,
        cost_estimate=cost(5.0),
        name="first_step",
    )(at, lh, ml, mr, rh, *tables)


def strength_of(parts, k):
    def total(m):
        a = [p[(m,) + k] for p in parts]
        return (a[0] + a[1]) + (a[2] + a[3])

    zeroth, first_moment = total(0), total(1)
    return DISSIPATION * zeroth * (first_moment / jnp.maximum(zeroth, MOMENT_FLOOR))


def second_kernel(
    at, e_ref, m0, m1, m2, m3, c_ref, u_ref, v_ref, w_ref, t_ref,
    out_ref, mom_ref, acc, s_scr, d_scr,
):
    first = at[0] * NFB
    acc[...] = jnp.zeros_like(acc)
    own = quad_spread(strength_of((m0, m1, m2, m3), (0,)))
    edge = quad_spread(strength_of((m0, m1, m2, m3), (1,)))
    for i, x in enumerate((edge[0],) + own + (edge[2],)):
        s_scr[i] = x

    def body(f, carry):
        freq = frequency_of(first + f)
        square = freq * freq
        for i in range(6):
            d_scr[i] = w_ref[i + 1] / (1.0 + s_scr[i] * square)
        def over(d, levels):
            levels = list(levels)

            def store(i, value):
                out_ref[i - 1, f, d] = value
                levels[i - 1] = levels[i - 1] + value

            advance(
                6,
                lambda i: e_ref[i, f, d] * d_scr[i],
                lambda i: c_ref[f, i + 1],
                lambda i: u_ref[1, i + 1],
                lambda i: v_ref[1, i + 1],
                twice(t_ref[0, d]),
                twice(t_ref[1, d]),
                store,
            )
            return tuple(levels)

        levels = lax.fori_loop(0, NQ, over, zeros(4), unroll=UNROLL)
        add_moments(acc, levels, lambda i: w_ref[i + 2], freq)
        return carry

    lax.fori_loop(0, NFB, body, 0)
    for m in range(2):
        mom_ref[m] = select4([quad_sum(acc[m, i]) for i in range(4)])


def second_step(at, e, moments, c, u, v, w, t):
    return pl.pallas_call(
        second_kernel,
        in_specs=[SM] + [VM] * 10,
        out_specs=[VM] * 2,
        out_shape=[
            jax.ShapeDtypeStruct((4, NFB, NQ, ROWS, LANES), F32),
            jax.ShapeDtypeStruct((2, ROWS, LANES), F32),
        ],
        scratch_shapes=[
            pltpu.VMEM((2, 4, ROWS, LANES), F32),
            pltpu.VMEM((6, ROWS, LANES), F32),
            pltpu.VMEM((6, ROWS, LANES), F32),
        ],
        compiler_params=PARAMS,
        cost_estimate=cost(3.5),
        name="second_step",
    )(at, e, *moments, c, u, v, w, t)


def unpack_kernel(e_ref, out_ref):
    def body(f, carry):
        for d in range(NQ):
            out = quad_transpose([e_ref[c, f, d] for c in range(4)])
            for q in range(4):
                store_rows(out_ref, (f, d + NQ * q), out[q])
        return carry

    lax.fori_loop(0, NFB, body, 0)


def unpack(e):
    return pl.pallas_call(
        unpack_kernel,
        in_specs=[VM],
        out_specs=VM,
        out_shape=jax.ShapeDtypeStruct((NFB, ND, ROWS, LANES), F32),
        compiler_params=PARAMS,
        cost_estimate=cost(2.0),
        name="unpack",
    )(e)


def last_kernel(at, e_ref, w_ref, m0, m1, m2, m3, out_hbm, buf, s_scr, sem):
    first = at[0] * NFB
    store_rows(s_scr, (0,), strength_of((m0, m1, m2, m3), ()))
    store_rows(s_scr, (1,), select4([w_ref[i] for i in range(2, 6)]))

    def save(f):
        return pltpu.make_async_copy(buf.at[f], out_hbm.at[f], sem.at[f])

    def body(f, carry):
        freq = frequency_of(first + f)
        damp = s_scr[1] / (1.0 + s_scr[0] * (freq * freq))
        for d in range(ND):
            buf[f, d] = e_ref[f, d] * damp
        save(f).start()
        return carry

    lax.fori_loop(0, NFB, body, 0)
    for f in range(NFB):
        save(f).wait()


def last_step(at, e, w, moments):
    return pl.pallas_call(
        last_kernel,
        in_specs=[SM] + [VM] * 6,
        out_specs=HB,
        out_shape=jax.ShapeDtypeStruct((NFB, ND, ROWS, LANES), F32),
        scratch_shapes=[
            pltpu.VMEM((NFB, ND, ROWS, LANES), F32),
            pltpu.VMEM((2, ROWS, LANES), F32),
            pltpu.SemaphoreType.DMA((NFB,)),
        ],
        compiler_params=PARAMS,
        cost_estimate=cost(1.5),
        name="last_step",
    )(at, e, w, *moments)


RIGHT = [(i, (i + 1) % PTS) for i in range(PTS)]
LEFT = [(b, a) for a, b in RIGHT]


def band_parts(x):
    return [x] + [
        lax.ppermute(x, "band", [(i, i ^ k) for i in range(BANDS)]) for k in range(1, BANDS)
    ]


def per_device(spectra, currents, bathymetry, sea_mask):
    forcing = jnp.concatenate(
        [
            currents.reshape(3 * SUBSTEPS, 4, LANES),
            bathymetry[None],
            sea_mask.astype(F32)[None],
        ],
        0,
    ).reshape(4 * FIELDS, LANES)
    at = jnp.stack([lax.axis_index("band"), lax.axis_index("pts")]).astype(jnp.int32)
    windows = forcing_windows(forcing)
    ml, mr = pack(jnp.transpose(spectra, (1, 2, 0, 3)))
    windows = lax.all_to_all(windows, ("band", "pts"), 0, 0, tiled=True)
    lh = lax.ppermute(mr, "pts", RIGHT)
    rh = lax.ppermute(ml, "pts", LEFT)
    turn = turns()
    c, u, v, w, depth = speeds(at, windows)
    e, moments = first_step(at, lh, ml, mr, rh, (c, u, v, w, turn))
    c = second_speeds(at, depth)
    e, moments = second_step(at, e, band_parts(moments), c, u, v, w, turn)
    return jnp.transpose(last_step(at, unpack(e), w, band_parts(moments)), (2, 0, 1, 3))


def solution(mesh):
    in_specs = (
        P(None, "band", None, "pts"),
        P(None, None, "band", "pts"),
        P("band", "pts"),
        P("band", "pts"),
    )
    out_specs = P(None, "band", None, "pts")
    return jax.shard_map(
        per_device, mesh=mesh, in_specs=in_specs, out_specs=out_specs, check_vma=False
    )
```

```python
import math

import jax
import jax.numpy as jnp
from jax import lax
from jax.experimental import pallas as pl
from jax.experimental.pallas import tpu as pltpu
from jax.sharding import PartitionSpec as P

GRAVITY = 9.81
COURANT = 0.02
DISSIPATION = 1.0
MOMENT_FLOOR = 0.01
FREQ_FIRST = 0.035
FREQ_STEP = 1.1
BAND_WIDTH = 0.0955
ND = 36
NQ = 9
NFB = 9
ROWS = 16
BANDS = 4
PTS = 32
SUBSTEPS = 2
FIELDS = 8
LANES = 128
F32 = jnp.float32
VMEM_LIMIT = 40 * 1024 * 1024
VM = pl.BlockSpec(memory_space=pltpu.VMEM)
SM = pl.BlockSpec(memory_space=pltpu.SMEM)
HB = pl.BlockSpec(memory_space=pltpu.HBM)
PARAMS = pltpu.CompilerParams(vmem_limit_bytes=VMEM_LIMIT)


def lane_group():
    return lax.broadcasted_iota(jnp.int32, (ROWS, LANES), 1) & 3


def lroll(x, shift):
    return pltpu.roll(x, shift % LANES, 1)


def lane_swap(x, distance):
    index = lax.broadcasted_iota(jnp.int32, x.shape, 1) ^ distance
    return jnp.take_along_axis(x, index, axis=1)


def quad_transpose(a):
    lane = lane_group()

    def exchange(x, y, distance):
        low = (lane & distance) == 0
        t = lane_swap(jnp.where(low, y, x), distance)
        return jnp.where(low, x, t), jnp.where(low, t, y)

    b0, b2 = exchange(a[0], a[2], 2)
    b1, b3 = exchange(a[1], a[3], 2)
    o0, o1 = exchange(b0, b1, 1)
    o2, o3 = exchange(b2, b3, 1)
    return o0, o1, o2, o3


def quad_spread(x):
    lane = lax.broadcasted_iota(jnp.int32, x.shape, 1)
    return tuple(jnp.take_along_axis(x, (lane & ~3) + k, axis=1) for k in range(4))


def quad_sum(x):
    x = x + lane_swap(x, 1)
    return x + lane_swap(x, 2)


def select4(x):
    lane = lane_group()
    return jnp.where(
        lane < 2, jnp.where(lane == 0, x[0], x[1]), jnp.where(lane == 2, x[2], x[3])
    )


def frequency_of(index):
    return FREQ_FIRST * jnp.exp(
        jnp.full((ROWS, LANES), index, jnp.int32).astype(F32) * math.log(FREQ_STEP)
    )


def edge_shifts(pts):
    left = jnp.where(pts == 0, 4, 0)
    right = jnp.where(pts == PTS - 1, LANES - 4, 0)
    return left, right


def cost(microseconds):
    return pl.CostEstimate(
        flops=0, transcendentals=0, bytes_accessed=int(microseconds * 3.0e6)
    )


def loop(count, body):
    lax.fori_loop(0, count, lambda i, carry: (body(i), carry)[1], 0)


def load_rows(ref, lead):
    return jnp.concatenate(
        [ref[lead + (pl.ds(parity, 8, stride=2), slice(None))] for parity in range(2)], axis=0
    )


def store_rows(ref, lead, value):
    for parity in range(2):
        ref[lead + (pl.ds(parity, 8, stride=2), slice(None))] = value[8 * parity : 8 * parity + 8]


def pack_kernel(e_hbm, ml_ref, mr_ref, buf, sem):
    def load(f):
        return pltpu.make_async_copy(e_hbm.at[f], buf.at[f], sem.at[f])

    for f in range(NFB):
        load(f).start()

    def body(f):
        load(f).wait()
        for d in range(NQ):
            out = quad_transpose([load_rows(buf, (f, d + NQ * q)) for q in range(4)])
            ml_ref[0, f, d] = out[0]
            ml_ref[1, f, d] = out[1]
            mr_ref[0, f, d] = out[2]
            mr_ref[1, f, d] = out[3]

    loop(NFB, body)


def pack(spectra):
    shape = jax.ShapeDtypeStruct((2, NFB, NQ, ROWS, LANES), F32)
    return pl.pallas_call(
        pack_kernel,
        in_specs=[HB],
        out_specs=[VM, VM],
        out_shape=[shape, shape],
        scratch_shapes=[
            pltpu.VMEM((NFB, ND, ROWS, LANES), F32),
            pltpu.SemaphoreType.DMA((NFB,)),
        ],
        compiler_params=pltpu.CompilerParams(vmem_limit_bytes=50 * 1024 * 1024),
        cost_estimate=cost(2.5),
        name="pack",
    )(spectra)


def exact_dot(a, b, dims):
    return lax.dot_general(
        a, b, (dims, ((), ())), precision=lax.Precision.HIGHEST, preferred_element_type=F32
    )


def forcing_kernel(own, out_ref):
    shape = (8 * PTS, LANES)
    place = lax.broadcasted_iota(jnp.int32, shape, 0)
    wanted = (4 * (place & (PTS - 1)) + (place >> 5) + (LANES - 2)) & (LANES - 1)
    pick = (lax.broadcasted_iota(jnp.int32, shape, 1) == wanted).astype(F32)
    x = exact_dot(pick, own[...], ((1,), (1,)))
    for h in range(2):
        row = jnp.concatenate(
            [x[PTS * (4 * h + k) : PTS * (4 * h + k) + PTS] for k in range(4)], axis=1
        )
        for band in range(BANDS):
            out_ref[PTS * band : PTS * band + PTS, h, :] = row


def forcing_windows(forcing):
    return pl.pallas_call(
        forcing_kernel,
        in_specs=[VM],
        out_specs=VM,
        out_shape=jax.ShapeDtypeStruct((BANDS * PTS, 2, LANES), F32),
        compiler_params=PARAMS,
        cost_estimate=cost(0.8),
        name="forcing",
    )(forcing)


def spread_columns(x, y):
    a, b = quad_spread(x), quad_spread(y)
    return (b[2], b[3]) + a + (b[0], b[1])


def celerities(first, h_ref, c_ref):
    def body(third):
        for f in [3 * third + k for k in range(3)]:
            angular = (2.0 * math.pi) * frequency_of(first + f)
            deep = angular * angular / GRAVITY
            speed = []
            for part in range(2):
                height = h_ref[part]
                wavenumber = deep / jnp.sqrt(jnp.tanh(deep * height))
                q = 2.0 * wavenumber * height
                ratio = 2.0 * q * jnp.exp(-q) / (1.0 - jnp.exp(-2.0 * q))
                speed.append((0.5 * COURANT) * (1.0 + ratio) * angular / wavenumber)
            for i, x in enumerate(spread_columns(*speed)):
                c_ref[f, i] = x

    loop(NFB // 3, body)


def speed_kernel(at, win, after, c_ref, u_ref, v_ref, w_ref, h_ref, f_scr, h_scr):
    left, right = edge_shifts(at[1])
    shape = (PTS, LANES)
    place = lax.broadcasted_iota(jnp.int32, shape, 0)
    spread = ((lax.broadcasted_iota(jnp.int32, shape, 1) >> 2) == place).astype(F32)
    for band in range(BANDS):
        for h in range(2):
            block = win[PTS * band : PTS * band + PTS, h, :]
            fields = exact_dot(block, spread, ((0,), (0,)))
            for k in range(4):
                i = 4 * h + k
                part = fields[32 * k : 32 * k + 32]
                if i < 2:
                    part = pltpu.roll(part, left, 1)
                if i >= 6:
                    part = pltpu.roll(part, right, 1)
                for n in range(FIELDS):
                    f_scr[i, n, 4 * band : 4 * band + 4, :] = part[4 * n : 4 * n + 4]
    for i in range(8):
        w_ref[i] = load_rows(f_scr, (i, 7))
        for s in range(SUBSTEPS):
            u_ref[s, i] = COURANT * load_rows(f_scr, (i, 3 * s))
            v_ref[s, i] = COURANT * load_rows(f_scr, (i, 3 * s + 1))
    for s, ref in ((0, h_scr), (1, h_ref)):
        depth = [load_rows(f_scr, (i, 6)) + load_rows(f_scr, (i, 3 * s + 2)) for i in range(8)]
        ref[0] = select4(depth[2:6])
        ref[1] = select4([depth[6], depth[7], depth[0], depth[1]])
    celerities(at[0] * NFB, h_scr, c_ref)


def speeds(at, windows, after):
    return pl.pallas_call(
        speed_kernel,
        in_specs=[SM, VM, pl.BlockSpec(memory_space=pl.ANY)],
        out_specs=[VM] * 5,
        out_shape=[
            jax.ShapeDtypeStruct((NFB, 8, ROWS, LANES), F32),
            jax.ShapeDtypeStruct((SUBSTEPS, 8, ROWS, LANES), F32),
            jax.ShapeDtypeStruct((SUBSTEPS, 8, ROWS, LANES), F32),
            jax.ShapeDtypeStruct((8, ROWS, LANES), F32),
            jax.ShapeDtypeStruct((2, ROWS, LANES), F32),
        ],
        scratch_shapes=[
            pltpu.VMEM((8, FIELDS, ROWS, LANES), F32),
            pltpu.VMEM((2, ROWS, LANES), F32),
        ],
        compiler_params=PARAMS,
        cost_estimate=cost(2.0),
        name="speeds",
    )(at, windows, after)


def turn_kernel(t_ref):
    for d in range(NQ):
        angle = (d + NQ * lane_group()[0:8]).astype(F32) * (2.0 * math.pi / ND)
        t_ref[0, d] = jnp.cos(angle)
        t_ref[1, d] = jnp.sin(angle)


def turns():
    return pl.pallas_call(
        turn_kernel,
        out_specs=VM,
        out_shape=jax.ShapeDtypeStruct((2, NQ, 8, LANES), F32),
        compiler_params=PARAMS,
        cost_estimate=cost(0.5),
        name="turns",
    )()


def align_kernel(at, lh, rh, lo_ref, ro_ref):
    def shift(ref, amount):
        def body(f):
            for k in range(2):
                for d in range(NQ):
                    ref[k, f, d] = lroll(ref[k, f, d], amount)

        loop(NFB, body)

    @pl.when(at[1] == 0)
    def _():
        shift(lo_ref, 4)

    @pl.when(at[1] == PTS - 1)
    def _():
        shift(ro_ref, -4)


def align(at, lh, rh):
    shape = jax.ShapeDtypeStruct((2, NFB, NQ, ROWS, LANES), F32)
    return pl.pallas_call(
        align_kernel,
        in_specs=[SM, VM, VM],
        out_specs=[VM, VM],
        out_shape=[shape, shape],
        input_output_aliases={1: 0, 2: 1},
        compiler_params=PARAMS,
        cost_estimate=cost(1.0),
        name="align",
    )(at, lh, rh)


def second_speed_kernel(at, h_ref, c_ref):
    celerities(at[0] * NFB, h_ref, c_ref)


def second_speeds(at, h):
    return pl.pallas_call(
        second_speed_kernel,
        in_specs=[SM, VM],
        out_specs=VM,
        out_shape=jax.ShapeDtypeStruct((NFB, 8, ROWS, LANES), F32),
        compiler_params=PARAMS,
        cost_estimate=cost(1.5),
        name="second_speeds",
    )(at, h)


def row_flux(b):
    sub = lax.broadcasted_iota(jnp.int32, (8, LANES), 0)
    plus, minus = jnp.maximum(b, 0.0), jnp.minimum(b, 0.0)
    even = plus[0:8] + minus[8:16]
    odd = plus[8:16] + jnp.where(sub == 7, 0.0, pltpu.roll(minus[0:8], 7, 0))
    before = jnp.where(sub == 0, minus[0:8], pltpu.roll(odd, 1, 0))
    return jnp.concatenate([even - before, odd - even], axis=0)


def advance(count, energy, speed, current_x, current_y, cos, sin, store):
    plus = None
    entered = None
    part = None
    for i in range(count):
        e = energy(i)
        c = speed(i)
        a = (c * cos + current_x(i)) * e
        if plus is not None:
            crossed = plus + jnp.minimum(a, 0.0)
            if part is not None:
                store(i - 1, part - crossed)
            entered = crossed
        if 0 < i < count - 1:
            b = (c * sin + current_y(i)) * e
            part = e + entered - row_flux(b)
        plus = jnp.maximum(a, 0.0)


UNROLL = 9


def zeros(count):
    return tuple(jnp.zeros((ROWS, LANES), F32) for _ in range(count))


def twice(x):
    return jnp.concatenate([x, x], axis=0)


def add_moments(acc, levels, wet, freq):
    weight = (BAND_WIDTH * (2.0 * math.pi / ND)) * freq
    for i, level in enumerate(levels):
        t = level * wet(i) * weight
        acc[0, i] = acc[0, i] + t
        acc[1, i] = acc[1, i] + t * freq


def first_kernel(at, lh, ml, mr, rh, c_ref, u_ref, v_ref, w_ref, t_ref, out_ref, mom_ref, acc):
    first = at[0] * NFB
    acc[...] = jnp.zeros_like(acc)

    def body(f):
        def over(d, levels):
            levels = list(levels)

            def store(i, value):
                out_ref[i - 1, f, d] = value
                levels[i - 1] = levels[i - 1] + value

            def energy(i):
                return (lh, ml, mr, rh)[i // 2][i % 2, f, d] * w_ref[i]

            advance(
                8,
                energy,
                lambda i: c_ref[f, i],
                lambda i: u_ref[0, i],
                lambda i: v_ref[0, i],
                twice(t_ref[0, d]),
                twice(t_ref[1, d]),
                store,
            )
            return tuple(levels)

        levels = lax.fori_loop(0, NQ, over, zeros(6), unroll=UNROLL)
        add_moments(acc, levels, lambda i: w_ref[i + 1], frequency_of(first + f))

    loop(NFB, body)
    for m in range(2):
        sums = [quad_sum(acc[m, i]) for i in range(6)]
        mom_ref[m, 0] = select4(sums[1:5])
        mom_ref[m, 1] = jnp.where(lane_group() < 2, sums[0], sums[5])


def first_step(at, lh, ml, mr, rh, tables):
    return pl.pallas_call(
        first_kernel,
        in_specs=[SM] + [VM] * 9,
        out_specs=[VM] * 2,
        out_shape=[
            jax.ShapeDtypeStruct((6, NFB, NQ, ROWS, LANES), F32),
            jax.ShapeDtypeStruct((2, 2, ROWS, LANES), F32),
        ],
        scratch_shapes=[pltpu.VMEM((2, 6, ROWS, LANES), F32)],
        compiler_params=PARAMS,
        cost_estimate=cost(5.0),
        name="first_step",
    )(at, lh, ml, mr, rh, *tables)


def strength_of(parts, k):
    def total(m):
        a = [p[(m,) + k] for p in parts]
        return (a[0] + a[1]) + (a[2] + a[3])

    zeroth, first_moment = total(0), total(1)
    return DISSIPATION * zeroth * (first_moment / jnp.maximum(zeroth, MOMENT_FLOOR))


def second_kernel(
    at, e_ref, m0, m1, m2, m3, c_ref, u_ref, v_ref, w_ref, t_ref,
    out_ref, mom_ref, acc, s_scr, d_scr,
):
    first = at[0] * NFB
    acc[...] = jnp.zeros_like(acc)
    own = quad_spread(strength_of((m0, m1, m2, m3), (0,)))
    edge = quad_spread(strength_of((m0, m1, m2, m3), (1,)))
    for i, x in enumerate((edge[0],) + own + (edge[2],)):
        s_scr[i] = x

    def body(f, carry):
        freq = frequency_of(first + f)
        square = freq * freq
        for i in range(6):
            d_scr[i] = w_ref[i + 1] / (1.0 + s_scr[i] * square)
        def over(d, levels):
            levels = list(levels)

            def store(i, value):
                out_ref[i - 1, f, d] = value
                levels[i - 1] = levels[i - 1] + value

            advance(
                6,
                lambda i: e_ref[i, f, d] * d_scr[i],
                lambda i: c_ref[f, i + 1],
                lambda i: u_ref[1, i + 1],
                lambda i: v_ref[1, i + 1],
                twice(t_ref[0, d]),
                twice(t_ref[1, d]),
                store,
            )
            return tuple(levels)

        levels = lax.fori_loop(0, NQ, over, zeros(4), unroll=UNROLL)
        add_moments(acc, levels, lambda i: w_ref[i + 2], freq)
        return carry

    lax.fori_loop(0, NFB, body, 0)
    for m in range(2):
        mom_ref[m] = select4([quad_sum(acc[m, i]) for i in range(4)])


def second_step(at, e, moments, c, u, v, w, t):
    return pl.pallas_call(
        second_kernel,
        in_specs=[SM] + [VM] * 10,
        out_specs=[VM] * 2,
        out_shape=[
            jax.ShapeDtypeStruct((4, NFB, NQ, ROWS, LANES), F32),
            jax.ShapeDtypeStruct((2, ROWS, LANES), F32),
        ],
        scratch_shapes=[
            pltpu.VMEM((2, 4, ROWS, LANES), F32),
            pltpu.VMEM((6, ROWS, LANES), F32),
            pltpu.VMEM((6, ROWS, LANES), F32),
        ],
        compiler_params=PARAMS,
        cost_estimate=cost(3.5),
        name="second_step",
    )(at, e, *moments, c, u, v, w, t)


def unpack_kernel(e_ref, out_ref):
    def body(f, carry):
        for d in range(NQ):
            out = quad_transpose([e_ref[c, f, d] for c in range(4)])
            for q in range(4):
                store_rows(out_ref, (f, d + NQ * q), out[q])
        return carry

    lax.fori_loop(0, NFB, body, 0)


def unpack(e):
    return pl.pallas_call(
        unpack_kernel,
        in_specs=[VM],
        out_specs=VM,
        out_shape=jax.ShapeDtypeStruct((NFB, ND, ROWS, LANES), F32),
        compiler_params=PARAMS,
        cost_estimate=cost(2.0),
        name="unpack",
    )(e)


def last_kernel(at, e_ref, w_ref, m0, m1, m2, m3, out_hbm, buf, s_scr, sem):
    first = at[0] * NFB
    store_rows(s_scr, (0,), strength_of((m0, m1, m2, m3), ()))
    store_rows(s_scr, (1,), select4([w_ref[i] for i in range(2, 6)]))

    def save(f):
        return pltpu.make_async_copy(buf.at[f], out_hbm.at[f], sem.at[f])

    def body(f, carry):
        freq = frequency_of(first + f)
        damp = s_scr[1] / (1.0 + s_scr[0] * (freq * freq))
        for d in range(ND):
            buf[f, d] = e_ref[f, d] * damp
        save(f).start()
        return carry

    lax.fori_loop(0, NFB, body, 0)
    for f in range(NFB):
        save(f).wait()


def last_step(at, e, w, moments):
    return pl.pallas_call(
        last_kernel,
        in_specs=[SM] + [VM] * 6,
        out_specs=HB,
        out_shape=jax.ShapeDtypeStruct((NFB, ND, ROWS, LANES), F32),
        scratch_shapes=[
            pltpu.VMEM((NFB, ND, ROWS, LANES), F32),
            pltpu.VMEM((2, ROWS, LANES), F32),
            pltpu.SemaphoreType.DMA((NFB,)),
        ],
        compiler_params=PARAMS,
        cost_estimate=cost(1.5),
        name="last_step",
    )(at, e, w, *moments)


RIGHT = [(i, (i + 1) % PTS) for i in range(PTS)]
LEFT = [(b, a) for a, b in RIGHT]


def band_parts(x):
    far, middle, near = [
        lax.ppermute(x, "band", [(i, i ^ k) for i in range(BANDS)]) for k in (3, 2, 1)
    ]
    return [x, near, middle, far]


def per_device(spectra, currents, bathymetry, sea_mask):
    forcing = jnp.concatenate(
        [
            currents.reshape(3 * SUBSTEPS, 4, LANES),
            bathymetry[None],
            sea_mask.astype(F32)[None],
        ],
        0,
    ).reshape(4 * FIELDS, LANES)
    at = jnp.stack([lax.axis_index("band"), lax.axis_index("pts")]).astype(jnp.int32)
    windows = forcing_windows(forcing)
    ml, mr = pack(jnp.transpose(spectra, (1, 2, 0, 3)))
    windows = lax.all_to_all(windows, ("band", "pts"), 0, 0, tiled=True)
    lh = lax.ppermute(mr, "pts", RIGHT)
    rh = lax.ppermute(ml, "pts", LEFT)
    turn = turns()
    lh, rh = align(at, lh, rh)
    c, u, v, w, depth = speeds(at, windows, lh)
    e, moments = first_step(at, lh, ml, mr, rh, (c, u, v, w, turn))
    c = second_speeds(at, depth)
    e, moments = second_step(at, e, band_parts(moments), c, u, v, w, turn)
    return jnp.transpose(last_step(at, unpack(e), w, band_parts(moments)), (2, 0, 1, 3))


def solution(mesh):
    in_specs = (
        P(None, "band", None, "pts"),
        P(None, None, "band", "pts"),
        P("band", "pts"),
        P("band", "pts"),
    )
    out_specs = P(None, "band", None, "pts")
    return jax.shard_map(
        per_device, mesh=mesh, in_specs=in_specs, out_specs=out_specs, check_vma=False
    )
```

```python
import math

import jax
import jax.numpy as jnp
from jax import lax
from jax.experimental import pallas as pl
from jax.experimental.pallas import tpu as pltpu
from jax.sharding import PartitionSpec as P

GRAVITY = 9.81
COURANT = 0.02
DISSIPATION = 1.0
MOMENT_FLOOR = 0.01
FREQ_FIRST = 0.035
FREQ_STEP = 1.1
BAND_WIDTH = 0.0955
ND = 36
NQ = 9
NFB = 9
ROWS = 16
BANDS = 4
PTS = 32
SUBSTEPS = 2
FIELDS = 8
LANES = 128
F32 = jnp.float32
VMEM_LIMIT = 40 * 1024 * 1024
VM = pl.BlockSpec(memory_space=pltpu.VMEM)
SM = pl.BlockSpec(memory_space=pltpu.SMEM)
HB = pl.BlockSpec(memory_space=pltpu.HBM)
PARAMS = pltpu.CompilerParams(vmem_limit_bytes=VMEM_LIMIT)


def lane_group():
    return lax.broadcasted_iota(jnp.int32, (ROWS, LANES), 1) & 3


def lroll(x, shift):
    return pltpu.roll(x, shift % LANES, 1)


def lane_swap(x, distance):
    index = lax.broadcasted_iota(jnp.int32, x.shape, 1) ^ distance
    return jnp.take_along_axis(x, index, axis=1)


def quad_transpose(a):
    lane = lane_group()

    def exchange(x, y, distance):
        low = (lane & distance) == 0
        t = lane_swap(jnp.where(low, y, x), distance)
        return jnp.where(low, x, t), jnp.where(low, t, y)

    b0, b2 = exchange(a[0], a[2], 2)
    b1, b3 = exchange(a[1], a[3], 2)
    o0, o1 = exchange(b0, b1, 1)
    o2, o3 = exchange(b2, b3, 1)
    return o0, o1, o2, o3


def quad_spread(x):
    lane = lax.broadcasted_iota(jnp.int32, x.shape, 1)
    return tuple(jnp.take_along_axis(x, (lane & ~3) + k, axis=1) for k in range(4))


def quad_sum(x):
    x = x + lane_swap(x, 1)
    return x + lane_swap(x, 2)


def select4(x):
    lane = lane_group()
    return jnp.where(
        lane < 2, jnp.where(lane == 0, x[0], x[1]), jnp.where(lane == 2, x[2], x[3])
    )


def frequency_of(index):
    return FREQ_FIRST * jnp.exp(
        jnp.full((ROWS, LANES), index, jnp.int32).astype(F32) * math.log(FREQ_STEP)
    )


def edge_shifts(pts):
    left = jnp.where(pts == 0, 4, 0)
    right = jnp.where(pts == PTS - 1, LANES - 4, 0)
    return left, right


def cost(microseconds):
    return pl.CostEstimate(
        flops=0, transcendentals=0, bytes_accessed=int(microseconds * 3.0e6)
    )


def loop(count, body):
    lax.fori_loop(0, count, lambda i, carry: (body(i), carry)[1], 0)


def load_rows(ref, lead):
    return jnp.concatenate(
        [ref[lead + (pl.ds(parity, 8, stride=2), slice(None))] for parity in range(2)], axis=0
    )


def store_rows(ref, lead, value):
    for parity in range(2):
        ref[lead + (pl.ds(parity, 8, stride=2), slice(None))] = value[8 * parity : 8 * parity + 8]


def pack_kernel(e_hbm, ml_ref, mr_ref, buf, sem):
    def load(f):
        return pltpu.make_async_copy(e_hbm.at[f], buf.at[f], sem.at[f])

    for f in range(NFB):
        load(f).start()

    def body(f):
        load(f).wait()
        for d in range(NQ):
            out = quad_transpose([load_rows(buf, (f, d + NQ * q)) for q in range(4)])
            ml_ref[0, f, d] = out[0]
            ml_ref[1, f, d] = out[1]
            mr_ref[0, f, d] = out[2]
            mr_ref[1, f, d] = out[3]

    loop(NFB, body)


def pack(spectra):
    shape = jax.ShapeDtypeStruct((2, NFB, NQ, ROWS, LANES), F32)
    return pl.pallas_call(
        pack_kernel,
        in_specs=[HB],
        out_specs=[VM, VM],
        out_shape=[shape, shape],
        scratch_shapes=[
            pltpu.VMEM((NFB, ND, ROWS, LANES), F32),
            pltpu.SemaphoreType.DMA((NFB,)),
        ],
        compiler_params=pltpu.CompilerParams(vmem_limit_bytes=50 * 1024 * 1024),
        cost_estimate=cost(2.5),
        name="pack",
    )(spectra)


def exact_dot(a, b, dims):
    return lax.dot_general(
        a, b, (dims, ((), ())), precision=lax.Precision.HIGHEST, preferred_element_type=F32
    )


def forcing_kernel(own, out_ref):
    shape = (8 * PTS, LANES)
    place = lax.broadcasted_iota(jnp.int32, shape, 0)
    wanted = (4 * (place & (PTS - 1)) + (place >> 5) + (LANES - 2)) & (LANES - 1)
    pick = (lax.broadcasted_iota(jnp.int32, shape, 1) == wanted).astype(F32)
    x = exact_dot(pick, own[...], ((1,), (1,)))
    for h in range(2):
        row = jnp.concatenate(
            [x[PTS * (4 * h + k) : PTS * (4 * h + k) + PTS] for k in range(4)], axis=1
        )
        for band in range(BANDS):
            out_ref[PTS * band : PTS * band + PTS, h, :] = row


def forcing_windows(forcing):
    return pl.pallas_call(
        forcing_kernel,
        in_specs=[VM],
        out_specs=VM,
        out_shape=jax.ShapeDtypeStruct((BANDS * PTS, 2, LANES), F32),
        compiler_params=PARAMS,
        cost_estimate=cost(0.8),
        name="forcing",
    )(forcing)


def spread_columns(x, y):
    a, b = quad_spread(x), quad_spread(y)
    return (b[2], b[3]) + a + (b[0], b[1])


def celerities(first, h_ref, c_ref):
    def body(third):
        for f in [3 * third + k for k in range(3)]:
            angular = (2.0 * math.pi) * frequency_of(first + f)
            deep = angular * angular / GRAVITY
            speed = []
            for part in range(2):
                height = h_ref[part]
                wavenumber = deep / jnp.sqrt(jnp.tanh(deep * height))
                q = 2.0 * wavenumber * height
                ratio = 2.0 * q * jnp.exp(-q) / (1.0 - jnp.exp(-2.0 * q))
                speed.append((0.5 * COURANT) * (1.0 + ratio) * angular / wavenumber)
            for i, x in enumerate(spread_columns(*speed)):
                c_ref[f, i] = x

    loop(NFB // 3, body)


def speed_kernel(at, win, after, c_ref, u_ref, v_ref, w_ref, h_ref, f_scr, h_scr):
    left, right = edge_shifts(at[1])
    shape = (PTS, LANES)
    place = lax.broadcasted_iota(jnp.int32, shape, 0)
    spread = ((lax.broadcasted_iota(jnp.int32, shape, 1) >> 2) == place).astype(F32)
    for band in range(BANDS):
        for h in range(2):
            block = win[PTS * band : PTS * band + PTS, h, :]
            fields = exact_dot(block, spread, ((0,), (0,)))
            for k in range(4):
                i = 4 * h + k
                part = fields[32 * k : 32 * k + 32]
                if i < 2:
                    part = pltpu.roll(part, left, 1)
                if i >= 6:
                    part = pltpu.roll(part, right, 1)
                for n in range(FIELDS):
                    f_scr[i, n, 4 * band : 4 * band + 4, :] = part[4 * n : 4 * n + 4]
    for i in range(8):
        w_ref[i] = load_rows(f_scr, (i, 7))
        for s in range(SUBSTEPS):
            u_ref[s, i] = COURANT * load_rows(f_scr, (i, 3 * s))
            v_ref[s, i] = COURANT * load_rows(f_scr, (i, 3 * s + 1))
    for s, ref in ((0, h_scr), (1, h_ref)):
        depth = [load_rows(f_scr, (i, 6)) + load_rows(f_scr, (i, 3 * s + 2)) for i in range(8)]
        ref[0] = select4(depth[2:6])
        ref[1] = select4([depth[6], depth[7], depth[0], depth[1]])
    celerities(at[0] * NFB, h_scr, c_ref)


def speeds(at, windows, after):
    return pl.pallas_call(
        speed_kernel,
        in_specs=[SM, VM, pl.BlockSpec(memory_space=pl.ANY)],
        out_specs=[VM] * 5,
        out_shape=[
            jax.ShapeDtypeStruct((NFB, 8, ROWS, LANES), F32),
            jax.ShapeDtypeStruct((SUBSTEPS, 8, ROWS, LANES), F32),
            jax.ShapeDtypeStruct((SUBSTEPS, 8, ROWS, LANES), F32),
            jax.ShapeDtypeStruct((8, ROWS, LANES), F32),
            jax.ShapeDtypeStruct((2, ROWS, LANES), F32),
        ],
        scratch_shapes=[
            pltpu.VMEM((8, FIELDS, ROWS, LANES), F32),
            pltpu.VMEM((2, ROWS, LANES), F32),
        ],
        compiler_params=PARAMS,
        cost_estimate=cost(2.0),
        name="speeds",
    )(at, windows, after)


def turn_kernel(t_ref):
    for d in range(NQ):
        angle = (d + NQ * lane_group()[0:8]).astype(F32) * (2.0 * math.pi / ND)
        t_ref[0, d] = jnp.cos(angle)
        t_ref[1, d] = jnp.sin(angle)


def turns():
    return pl.pallas_call(
        turn_kernel,
        out_specs=VM,
        out_shape=jax.ShapeDtypeStruct((2, NQ, 8, LANES), F32),
        compiler_params=PARAMS,
        cost_estimate=cost(0.5),
        name="turns",
    )()


def align_kernel(at, lh, rh, lo_ref, ro_ref):
    def shift(ref, amount):
        def body(f):
            for k in range(2):
                for d in range(NQ):
                    ref[k, f, d] = lroll(ref[k, f, d], amount)

        loop(NFB, body)

    @pl.when(at[1] == 0)
    def _():
        shift(lo_ref, 4)

    @pl.when(at[1] == PTS - 1)
    def _():
        shift(ro_ref, -4)


def align(at, lh, rh):
    shape = jax.ShapeDtypeStruct((2, NFB, NQ, ROWS, LANES), F32)
    return pl.pallas_call(
        align_kernel,
        in_specs=[SM, VM, VM],
        out_specs=[VM, VM],
        out_shape=[shape, shape],
        input_output_aliases={1: 0, 2: 1},
        compiler_params=PARAMS,
        cost_estimate=cost(1.0),
        name="align",
    )(at, lh, rh)


def second_speed_kernel(at, h_ref, c_ref):
    celerities(at[0] * NFB, h_ref, c_ref)


def second_speeds(at, h):
    return pl.pallas_call(
        second_speed_kernel,
        in_specs=[SM, VM],
        out_specs=VM,
        out_shape=jax.ShapeDtypeStruct((NFB, 8, ROWS, LANES), F32),
        compiler_params=PARAMS,
        cost_estimate=cost(1.5),
        name="second_speeds",
    )(at, h)


def row_flux(b):
    sub = lax.broadcasted_iota(jnp.int32, (8, LANES), 0)
    plus, minus = jnp.maximum(b, 0.0), jnp.minimum(b, 0.0)
    even = plus[0:8] + minus[8:16]
    odd = plus[8:16] + jnp.where(sub == 7, 0.0, pltpu.roll(minus[0:8], 7, 0))
    before = jnp.where(sub == 0, minus[0:8], pltpu.roll(odd, 1, 0))
    return jnp.concatenate([even - before, odd - even], axis=0)


def advance(count, energy, speed, current_x, current_y, cos, sin, store):
    plus = None
    entered = None
    part = None
    for i in range(count):
        e = energy(i)
        c = speed(i)
        a = (c * cos + current_x(i)) * e
        if plus is not None:
            crossed = plus + jnp.minimum(a, 0.0)
            if part is not None:
                store(i - 1, part - crossed)
            entered = crossed
        if 0 < i < count - 1:
            b = (c * sin + current_y(i)) * e
            part = e + entered - row_flux(b)
        plus = jnp.maximum(a, 0.0)


UNROLL = 9


def zeros(count):
    return tuple(jnp.zeros((ROWS, LANES), F32) for _ in range(count))


def twice(x):
    return jnp.concatenate([x, x], axis=0)


def add_moments(acc, levels, wet, freq):
    weight = (BAND_WIDTH * (2.0 * math.pi / ND)) * freq
    for i, level in enumerate(levels):
        t = level * wet(i) * weight
        acc[0, i] = acc[0, i] + t
        acc[1, i] = acc[1, i] + t * freq


def first_kernel(at, lh, ml, mr, rh, c_ref, u_ref, v_ref, w_ref, t_ref, out_ref, mom_ref, acc):
    first = at[0] * NFB
    acc[...] = jnp.zeros_like(acc)

    def body(f):
        def over(d, levels):
            levels = list(levels)

            def store(i, value):
                out_ref[i - 1, f, d] = value
                levels[i - 1] = levels[i - 1] + value

            def energy(i):
                return (lh, ml, mr, rh)[i // 2][i % 2, f, d] * w_ref[i]

            advance(
                8,
                energy,
                lambda i: c_ref[f, i],
                lambda i: u_ref[0, i],
                lambda i: v_ref[0, i],
                twice(t_ref[0, d]),
                twice(t_ref[1, d]),
                store,
            )
            return tuple(levels)

        levels = lax.fori_loop(0, NQ, over, zeros(6), unroll=UNROLL)
        add_moments(acc, levels, lambda i: w_ref[i + 1], frequency_of(first + f))

    loop(NFB, body)
    for m in range(2):
        sums = [quad_sum(acc[m, i]) for i in range(6)]
        mom_ref[m, 0] = select4(sums[1:5])
        mom_ref[m, 1] = jnp.where(lane_group() < 2, sums[0], sums[5])


def first_step(at, lh, ml, mr, rh, tables):
    return pl.pallas_call(
        first_kernel,
        in_specs=[SM] + [VM] * 9,
        out_specs=[VM] * 2,
        out_shape=[
            jax.ShapeDtypeStruct((6, NFB, NQ, ROWS, LANES), F32),
            jax.ShapeDtypeStruct((2, 2, ROWS, LANES), F32),
        ],
        scratch_shapes=[pltpu.VMEM((2, 6, ROWS, LANES), F32)],
        compiler_params=PARAMS,
        cost_estimate=cost(5.0),
        name="first_step",
    )(at, lh, ml, mr, rh, *tables)


def strength_of(parts, k):
    def total(m):
        a = [p[(m,) + k] for p in parts]
        return (a[0] + a[1]) + (a[2] + a[3])

    zeroth, first_moment = total(0), total(1)
    return DISSIPATION * zeroth * (first_moment / jnp.maximum(zeroth, MOMENT_FLOOR))


def second_kernel(
    at, e_ref, m0, m1, m2, m3, c_ref, u_ref, v_ref, w_ref, t_ref,
    out_ref, mom_ref, acc, s_scr, d_scr,
):
    first = at[0] * NFB
    acc[...] = jnp.zeros_like(acc)
    own = quad_spread(strength_of((m0, m1, m2, m3), (0,)))
    edge = quad_spread(strength_of((m0, m1, m2, m3), (1,)))
    for i, x in enumerate((edge[0],) + own + (edge[2],)):
        s_scr[i] = x

    def body(f, carry):
        freq = frequency_of(first + f)
        square = freq * freq
        for i in range(6):
            d_scr[i] = w_ref[i + 1] / (1.0 + s_scr[i] * square)
        def over(d, levels):
            levels = list(levels)

            def store(i, value):
                out_ref[i - 1, f, d] = value
                levels[i - 1] = levels[i - 1] + value

            advance(
                6,
                lambda i: e_ref[i, f, d] * d_scr[i],
                lambda i: c_ref[f, i + 1],
                lambda i: u_ref[1, i + 1],
                lambda i: v_ref[1, i + 1],
                twice(t_ref[0, d]),
                twice(t_ref[1, d]),
                store,
            )
            return tuple(levels)

        levels = lax.fori_loop(0, NQ, over, zeros(4), unroll=UNROLL)
        add_moments(acc, levels, lambda i: w_ref[i + 2], freq)
        return carry

    lax.fori_loop(0, NFB, body, 0)
    for m in range(2):
        mom_ref[m] = select4([quad_sum(acc[m, i]) for i in range(4)])


def second_step(at, e, moments, c, u, v, w, t):
    return pl.pallas_call(
        second_kernel,
        in_specs=[SM] + [VM] * 10,
        out_specs=[VM] * 2,
        out_shape=[
            jax.ShapeDtypeStruct((4, NFB, NQ, ROWS, LANES), F32),
            jax.ShapeDtypeStruct((2, ROWS, LANES), F32),
        ],
        scratch_shapes=[
            pltpu.VMEM((2, 4, ROWS, LANES), F32),
            pltpu.VMEM((6, ROWS, LANES), F32),
            pltpu.VMEM((6, ROWS, LANES), F32),
        ],
        compiler_params=PARAMS,
        cost_estimate=cost(3.5),
        name="second_step",
    )(at, e, *moments, c, u, v, w, t)


def unpack_kernel(e_ref, out_ref):
    def body(f, carry):
        for d in range(NQ):
            out = quad_transpose([e_ref[c, f, d] for c in range(4)])
            for q in range(4):
                store_rows(out_ref, (f, d + NQ * q), out[q])
        return carry

    lax.fori_loop(0, NFB, body, 0)


def unpack(e):
    return pl.pallas_call(
        unpack_kernel,
        in_specs=[VM],
        out_specs=VM,
        out_shape=jax.ShapeDtypeStruct((NFB, ND, ROWS, LANES), F32),
        compiler_params=PARAMS,
        cost_estimate=cost(2.0),
        name="unpack",
    )(e)


def last_kernel(at, e_ref, w_ref, m0, m1, m2, m3, out_hbm, buf, s_scr, sem):
    first = at[0] * NFB
    store_rows(s_scr, (0,), strength_of((m0, m1, m2, m3), ()))
    store_rows(s_scr, (1,), select4([w_ref[i] for i in range(2, 6)]))

    def save(f):
        return pltpu.make_async_copy(buf.at[f], out_hbm.at[f], sem.at[f])

    def body(f, carry):
        freq = frequency_of(first + f)
        damp = s_scr[1] / (1.0 + s_scr[0] * (freq * freq))
        for d in range(ND):
            buf[f, d] = e_ref[f, d] * damp
        save(f).start()
        return carry

    lax.fori_loop(0, NFB, body, 0)
    for f in range(NFB):
        save(f).wait()


def last_step(at, e, w, moments):
    return pl.pallas_call(
        last_kernel,
        in_specs=[SM] + [VM] * 6,
        out_specs=HB,
        out_shape=jax.ShapeDtypeStruct((NFB, ND, ROWS, LANES), F32),
        scratch_shapes=[
            pltpu.VMEM((NFB, ND, ROWS, LANES), F32),
            pltpu.VMEM((2, ROWS, LANES), F32),
            pltpu.SemaphoreType.DMA((NFB,)),
        ],
        compiler_params=PARAMS,
        cost_estimate=cost(1.5),
        name="last_step",
    )(at, e, w, *moments)


RIGHT = [(i, (i + 1) % PTS) for i in range(PTS)]
LEFT = [(b, a) for a, b in RIGHT]


def band_parts(x):
    near, middle, far = [
        lax.ppermute(x, "band", [(i, i ^ k) for i in range(BANDS)]) for k in (1, 2, 3)
    ]
    return [x, near, far, middle]


def per_device(spectra, currents, bathymetry, sea_mask):
    forcing = jnp.concatenate(
        [
            currents.reshape(3 * SUBSTEPS, 4, LANES),
            bathymetry[None],
            sea_mask.astype(F32)[None],
        ],
        0,
    ).reshape(4 * FIELDS, LANES)
    at = jnp.stack([lax.axis_index("band"), lax.axis_index("pts")]).astype(jnp.int32)
    windows = forcing_windows(forcing)
    ml, mr = pack(jnp.transpose(spectra, (1, 2, 0, 3)))
    windows = lax.all_to_all(windows, ("band", "pts"), 0, 0, tiled=True)
    lh = lax.ppermute(mr, "pts", RIGHT)
    rh = lax.ppermute(ml, "pts", LEFT)
    turn = turns()
    lh, rh = align(at, lh, rh)
    c, u, v, w, depth = speeds(at, windows, lh)
    e, moments = first_step(at, lh, ml, mr, rh, (c, u, v, w, turn))
    c = second_speeds(at, depth)
    e, moments = second_step(at, e, band_parts(moments), c, u, v, w, turn)
    return jnp.transpose(last_step(at, unpack(e), w, band_parts(moments)), (2, 0, 1, 3))


def solution(mesh):
    in_specs = (
        P(None, "band", None, "pts"),
        P(None, None, "band", "pts"),
        P("band", "pts"),
        P("band", "pts"),
    )
    out_specs = P(None, "band", None, "pts")
    return jax.shard_map(
        per_device, mesh=mesh, in_specs=in_specs, out_specs=out_specs, check_vma=False
    )
```

```python
import math

import jax
import jax.numpy as jnp
from jax import lax
from jax.experimental import pallas as pl
from jax.experimental.pallas import tpu as pltpu
from jax.sharding import PartitionSpec as P

GRAVITY = 9.81
COURANT = 0.02
DISSIPATION = 1.0
MOMENT_FLOOR = 0.01
FREQ_FIRST = 0.035
FREQ_STEP = 1.1
BAND_WIDTH = 0.0955
ND = 36
NQ = 9
NFB = 9
ROWS = 16
BANDS = 4
PTS = 32
SUBSTEPS = 2
FIELDS = 8
LANES = 128
F32 = jnp.float32
VMEM_LIMIT = 40 * 1024 * 1024
VM = pl.BlockSpec(memory_space=pltpu.VMEM)
SM = pl.BlockSpec(memory_space=pltpu.SMEM)
HB = pl.BlockSpec(memory_space=pltpu.HBM)
PARAMS = pltpu.CompilerParams(vmem_limit_bytes=VMEM_LIMIT)


def lane_group():
    return lax.broadcasted_iota(jnp.int32, (ROWS, LANES), 1) & 3


def lroll(x, shift):
    return pltpu.roll(x, shift % LANES, 1)


def lane_swap(x, distance):
    index = lax.broadcasted_iota(jnp.int32, x.shape, 1) ^ distance
    return jnp.take_along_axis(x, index, axis=1)


def quad_transpose(a):
    lane = lane_group()

    def exchange(x, y, distance):
        low = (lane & distance) == 0
        t = lane_swap(jnp.where(low, y, x), distance)
        return jnp.where(low, x, t), jnp.where(low, t, y)

    b0, b2 = exchange(a[0], a[2], 2)
    b1, b3 = exchange(a[1], a[3], 2)
    o0, o1 = exchange(b0, b1, 1)
    o2, o3 = exchange(b2, b3, 1)
    return o0, o1, o2, o3


def quad_spread(x):
    lane = lax.broadcasted_iota(jnp.int32, x.shape, 1)
    return tuple(jnp.take_along_axis(x, (lane & ~3) + k, axis=1) for k in range(4))


def quad_sum(x):
    x = x + lane_swap(x, 1)
    return x + lane_swap(x, 2)


def select4(x):
    lane = lane_group()
    return jnp.where(
        lane < 2, jnp.where(lane == 0, x[0], x[1]), jnp.where(lane == 2, x[2], x[3])
    )


def frequency_of(index):
    return FREQ_FIRST * jnp.exp(
        jnp.full((ROWS, LANES), index, jnp.int32).astype(F32) * math.log(FREQ_STEP)
    )


def edge_shifts(pts):
    left = jnp.where(pts == 0, 4, 0)
    right = jnp.where(pts == PTS - 1, LANES - 4, 0)
    return left, right


def cost(microseconds):
    return pl.CostEstimate(
        flops=0, transcendentals=0, bytes_accessed=int(microseconds * 3.0e6)
    )


def loop(count, body):
    lax.fori_loop(0, count, lambda i, carry: (body(i), carry)[1], 0)


def load_rows(ref, lead):
    return jnp.concatenate(
        [ref[lead + (pl.ds(parity, 8, stride=2), slice(None))] for parity in range(2)], axis=0
    )


def store_rows(ref, lead, value):
    for parity in range(2):
        ref[lead + (pl.ds(parity, 8, stride=2), slice(None))] = value[8 * parity : 8 * parity + 8]


def pack_kernel(e_hbm, ml_ref, mr_ref, buf, sem):
    def load(f):
        return pltpu.make_async_copy(e_hbm.at[f], buf.at[f], sem.at[f])

    for f in range(NFB):
        load(f).start()

    def body(f):
        load(f).wait()
        for d in range(NQ):
            out = quad_transpose([load_rows(buf, (f, d + NQ * q)) for q in range(4)])
            ml_ref[0, f, d] = out[0]
            ml_ref[1, f, d] = out[1]
            mr_ref[0, f, d] = out[2]
            mr_ref[1, f, d] = out[3]

    loop(NFB, body)


def pack(spectra):
    shape = jax.ShapeDtypeStruct((2, NFB, NQ, ROWS, LANES), F32)
    return pl.pallas_call(
        pack_kernel,
        in_specs=[HB],
        out_specs=[VM, VM],
        out_shape=[shape, shape],
        scratch_shapes=[
            pltpu.VMEM((NFB, ND, ROWS, LANES), F32),
            pltpu.SemaphoreType.DMA((NFB,)),
        ],
        compiler_params=pltpu.CompilerParams(vmem_limit_bytes=52 * 1024 * 1024),
        cost_estimate=cost(2.5),
        name="pack",
    )(spectra)


def exact_dot(a, b, dims):
    return lax.dot_general(
        a, b, (dims, ((), ())), precision=lax.Precision.HIGHEST, preferred_element_type=F32
    )


def forcing_kernel(own, out_ref):
    shape = (8 * PTS, LANES)
    place = lax.broadcasted_iota(jnp.int32, shape, 0)
    wanted = (4 * (place & (PTS - 1)) + (place >> 5) + (LANES - 2)) & (LANES - 1)
    pick = (lax.broadcasted_iota(jnp.int32, shape, 1) == wanted).astype(F32)
    x = exact_dot(pick, own[...], ((1,), (1,)))
    for h in range(2):
        row = jnp.concatenate(
            [x[PTS * (4 * h + k) : PTS * (4 * h + k) + PTS] for k in range(4)], axis=1
        )
        for band in range(BANDS):
            out_ref[PTS * band : PTS * band + PTS, h, :] = row


def forcing_windows(forcing):
    return pl.pallas_call(
        forcing_kernel,
        in_specs=[VM],
        out_specs=VM,
        out_shape=jax.ShapeDtypeStruct((BANDS * PTS, 2, LANES), F32),
        compiler_params=PARAMS,
        cost_estimate=cost(0.8),
        name="forcing",
    )(forcing)


def spread_columns(x, y):
    a, b = quad_spread(x), quad_spread(y)
    return (b[2], b[3]) + a + (b[0], b[1])


def celerities(first, h_ref, c_ref):
    for f in range(NFB):
        angular = (2.0 * math.pi) * frequency_of(first + f)
        deep = angular * angular / GRAVITY
        speed = []
        for part in range(2):
            height = h_ref[part]
            wavenumber = deep / jnp.sqrt(jnp.tanh(deep * height))
            q = 2.0 * wavenumber * height
            ratio = 2.0 * q * jnp.exp(-q) / (1.0 - jnp.exp(-2.0 * q))
            speed.append((0.5 * COURANT) * (1.0 + ratio) * angular / wavenumber)
        for i, x in enumerate(spread_columns(*speed)):
            c_ref[f, i] = x


def speed_kernel(at, win, after, c_ref, u_ref, v_ref, w_ref, h_ref, f_scr, h_scr):
    left, right = edge_shifts(at[1])
    shape = (PTS, LANES)
    place = lax.broadcasted_iota(jnp.int32, shape, 0)
    spread = ((lax.broadcasted_iota(jnp.int32, shape, 1) >> 2) == place).astype(F32)
    for band in range(BANDS):
        for h in range(2):
            block = win[PTS * band : PTS * band + PTS, h, :]
            fields = exact_dot(block, spread, ((0,), (0,)))
            for k in range(4):
                i = 4 * h + k
                part = fields[32 * k : 32 * k + 32]
                if i < 2:
                    part = pltpu.roll(part, left, 1)
                if i >= 6:
                    part = pltpu.roll(part, right, 1)
                for n in range(FIELDS):
                    f_scr[i, n, 4 * band : 4 * band + 4, :] = part[4 * n : 4 * n + 4]
    for i in range(8):
        w_ref[i] = load_rows(f_scr, (i, 7))
        for s in range(SUBSTEPS):
            u_ref[s, i] = COURANT * load_rows(f_scr, (i, 3 * s))
            v_ref[s, i] = COURANT * load_rows(f_scr, (i, 3 * s + 1))
    for s, ref in ((0, h_scr), (1, h_ref)):
        depth = [load_rows(f_scr, (i, 6)) + load_rows(f_scr, (i, 3 * s + 2)) for i in range(8)]
        ref[0] = select4(depth[2:6])
        ref[1] = select4([depth[6], depth[7], depth[0], depth[1]])
    celerities(at[0] * NFB, h_scr, c_ref)


def speeds(at, windows, after):
    return pl.pallas_call(
        speed_kernel,
        in_specs=[SM, VM, pl.BlockSpec(memory_space=pl.ANY)],
        out_specs=[VM] * 5,
        out_shape=[
            jax.ShapeDtypeStruct((NFB, 8, ROWS, LANES), F32),
            jax.ShapeDtypeStruct((SUBSTEPS, 8, ROWS, LANES), F32),
            jax.ShapeDtypeStruct((SUBSTEPS, 8, ROWS, LANES), F32),
            jax.ShapeDtypeStruct((8, ROWS, LANES), F32),
            jax.ShapeDtypeStruct((2, ROWS, LANES), F32),
        ],
        scratch_shapes=[
            pltpu.VMEM((8, FIELDS, ROWS, LANES), F32),
            pltpu.VMEM((2, ROWS, LANES), F32),
        ],
        compiler_params=PARAMS,
        cost_estimate=cost(2.0),
        name="speeds",
    )(at, windows, after)


def turn_kernel(t_ref):
    for d in range(NQ):
        angle = (d + NQ * lane_group()[0:8]).astype(F32) * (2.0 * math.pi / ND)
        t_ref[0, d] = jnp.cos(angle)
        t_ref[1, d] = jnp.sin(angle)


def turns():
    return pl.pallas_call(
        turn_kernel,
        out_specs=VM,
        out_shape=jax.ShapeDtypeStruct((2, NQ, 8, LANES), F32),
        compiler_params=PARAMS,
        cost_estimate=cost(0.5),
        name="turns",
    )()


def align_kernel(at, lh, rh, lo_ref, ro_ref):
    def shift(ref, amount):
        def body(f):
            for k in range(2):
                for d in range(NQ):
                    ref[k, f, d] = lroll(ref[k, f, d], amount)

        loop(NFB, body)

    @pl.when(at[1] == 0)
    def _():
        shift(lo_ref, 4)

    @pl.when(at[1] == PTS - 1)
    def _():
        shift(ro_ref, -4)


def align(at, lh, rh):
    shape = jax.ShapeDtypeStruct((2, NFB, NQ, ROWS, LANES), F32)
    return pl.pallas_call(
        align_kernel,
        in_specs=[SM, VM, VM],
        out_specs=[VM, VM],
        out_shape=[shape, shape],
        input_output_aliases={1: 0, 2: 1},
        compiler_params=PARAMS,
        cost_estimate=cost(1.0),
        name="align",
    )(at, lh, rh)


def second_speed_kernel(at, h_ref, c_ref):
    celerities(at[0] * NFB, h_ref, c_ref)


def second_speeds(at, h):
    return pl.pallas_call(
        second_speed_kernel,
        in_specs=[SM, VM],
        out_specs=VM,
        out_shape=jax.ShapeDtypeStruct((NFB, 8, ROWS, LANES), F32),
        compiler_params=PARAMS,
        cost_estimate=cost(1.5),
        name="second_speeds",
    )(at, h)


def row_flux(b):
    sub = lax.broadcasted_iota(jnp.int32, (8, LANES), 0)
    plus, minus = jnp.maximum(b, 0.0), jnp.minimum(b, 0.0)
    even = plus[0:8] + minus[8:16]
    odd = plus[8:16] + jnp.where(sub == 7, 0.0, pltpu.roll(minus[0:8], 7, 0))
    before = jnp.where(sub == 0, minus[0:8], pltpu.roll(odd, 1, 0))
    return jnp.concatenate([even - before, odd - even], axis=0)


def advance(count, energy, speed, current_x, current_y, cos, sin, store):
    plus = None
    entered = None
    part = None
    for i in range(count):
        e = energy(i)
        c = speed(i)
        a = (c * cos + current_x(i)) * e
        if plus is not None:
            crossed = plus + jnp.minimum(a, 0.0)
            if part is not None:
                store(i - 1, part - crossed)
            entered = crossed
        if 0 < i < count - 1:
            b = (c * sin + current_y(i)) * e
            part = e + entered - row_flux(b)
        plus = jnp.maximum(a, 0.0)


UNROLL = 9


def zeros(count):
    return tuple(jnp.zeros((ROWS, LANES), F32) for _ in range(count))


def twice(x):
    return jnp.concatenate([x, x], axis=0)


def add_moments(acc, levels, wet, freq):
    weight = (BAND_WIDTH * (2.0 * math.pi / ND)) * freq
    for i, level in enumerate(levels):
        t = level * wet(i) * weight
        acc[0, i] = acc[0, i] + t
        acc[1, i] = acc[1, i] + t * freq


def first_kernel(at, lh, ml, mr, rh, c_ref, u_ref, v_ref, w_ref, t_ref, out_ref, mom_ref, acc):
    first = at[0] * NFB
    acc[...] = jnp.zeros_like(acc)

    def body(f):
        def over(d, levels):
            levels = list(levels)

            def store(i, value):
                out_ref[i - 1, f, d] = value
                levels[i - 1] = levels[i - 1] + value

            def energy(i):
                return (lh, ml, mr, rh)[i // 2][i % 2, f, d] * w_ref[i]

            advance(
                8,
                energy,
                lambda i: c_ref[f, i],
                lambda i: u_ref[0, i],
                lambda i: v_ref[0, i],
                twice(t_ref[0, d]),
                twice(t_ref[1, d]),
                store,
            )
            return tuple(levels)

        levels = lax.fori_loop(0, NQ, over, zeros(6), unroll=UNROLL)
        add_moments(acc, levels, lambda i: w_ref[i + 1], frequency_of(first + f))

    loop(NFB, body)
    for m in range(2):
        sums = [quad_sum(acc[m, i]) for i in range(6)]
        mom_ref[m, 0] = select4(sums[1:5])
        mom_ref[m, 1] = jnp.where(lane_group() < 2, sums[0], sums[5])


def first_step(at, lh, ml, mr, rh, tables):
    return pl.pallas_call(
        first_kernel,
        in_specs=[SM] + [VM] * 9,
        out_specs=[VM] * 2,
        out_shape=[
            jax.ShapeDtypeStruct((6, NFB, NQ, ROWS, LANES), F32),
            jax.ShapeDtypeStruct((2, 2, ROWS, LANES), F32),
        ],
        scratch_shapes=[pltpu.VMEM((2, 6, ROWS, LANES), F32)],
        compiler_params=PARAMS,
        cost_estimate=cost(5.0),
        name="first_step",
    )(at, lh, ml, mr, rh, *tables)


def strength_of(parts, k):
    def total(m):
        a = [p[(m,) + k] for p in parts]
        return (a[0] + a[1]) + (a[2] + a[3])

    zeroth, first_moment = total(0), total(1)
    return DISSIPATION * zeroth * (first_moment / jnp.maximum(zeroth, MOMENT_FLOOR))


def second_kernel(
    at, e_ref, m0, m1, m2, m3, c_ref, u_ref, v_ref, w_ref, t_ref,
    out_ref, mom_ref, acc, s_scr, d_scr,
):
    first = at[0] * NFB
    acc[...] = jnp.zeros_like(acc)
    own = quad_spread(strength_of((m0, m1, m2, m3), (0,)))
    edge = quad_spread(strength_of((m0, m1, m2, m3), (1,)))
    for i, x in enumerate((edge[0],) + own + (edge[2],)):
        s_scr[i] = x

    def body(f, carry):
        freq = frequency_of(first + f)
        square = freq * freq
        for i in range(6):
            d_scr[i] = w_ref[i + 1] / (1.0 + s_scr[i] * square)
        def over(d, levels):
            levels = list(levels)

            def store(i, value):
                out_ref[i - 1, f, d] = value
                levels[i - 1] = levels[i - 1] + value

            advance(
                6,
                lambda i: e_ref[i, f, d] * d_scr[i],
                lambda i: c_ref[f, i + 1],
                lambda i: u_ref[1, i + 1],
                lambda i: v_ref[1, i + 1],
                twice(t_ref[0, d]),
                twice(t_ref[1, d]),
                store,
            )
            return tuple(levels)

        levels = lax.fori_loop(0, NQ, over, zeros(4), unroll=UNROLL)
        add_moments(acc, levels, lambda i: w_ref[i + 2], freq)
        return carry

    lax.fori_loop(0, NFB, body, 0)
    for m in range(2):
        mom_ref[m] = select4([quad_sum(acc[m, i]) for i in range(4)])


def second_step(at, e, moments, c, u, v, w, t):
    return pl.pallas_call(
        second_kernel,
        in_specs=[SM] + [VM] * 10,
        out_specs=[VM] * 2,
        out_shape=[
            jax.ShapeDtypeStruct((4, NFB, NQ, ROWS, LANES), F32),
            jax.ShapeDtypeStruct((2, ROWS, LANES), F32),
        ],
        scratch_shapes=[
            pltpu.VMEM((2, 4, ROWS, LANES), F32),
            pltpu.VMEM((6, ROWS, LANES), F32),
            pltpu.VMEM((6, ROWS, LANES), F32),
        ],
        compiler_params=PARAMS,
        cost_estimate=cost(3.5),
        name="second_step",
    )(at, e, *moments, c, u, v, w, t)


def unpack_kernel(e_ref, out_ref):
    def body(f, carry):
        for d in range(NQ):
            out = quad_transpose([e_ref[c, f, d] for c in range(4)])
            for q in range(4):
                store_rows(out_ref, (f, d + NQ * q), out[q])
        return carry

    lax.fori_loop(0, NFB, body, 0)


def unpack(e):
    return pl.pallas_call(
        unpack_kernel,
        in_specs=[VM],
        out_specs=VM,
        out_shape=jax.ShapeDtypeStruct((NFB, ND, ROWS, LANES), F32),
        compiler_params=PARAMS,
        cost_estimate=cost(2.0),
        name="unpack",
    )(e)


def last_kernel(at, e_ref, w_ref, m0, m1, m2, m3, out_hbm, buf, s_scr, sem):
    first = at[0] * NFB
    store_rows(s_scr, (0,), strength_of((m0, m1, m2, m3), ()))
    store_rows(s_scr, (1,), select4([w_ref[i] for i in range(2, 6)]))

    def save(f):
        return pltpu.make_async_copy(buf.at[f], out_hbm.at[f], sem.at[f])

    def body(f, carry):
        freq = frequency_of(first + f)
        damp = s_scr[1] / (1.0 + s_scr[0] * (freq * freq))
        for d in range(ND):
            buf[f, d] = e_ref[f, d] * damp
        save(f).start()
        return carry

    lax.fori_loop(0, NFB, body, 0)
    for f in range(NFB):
        save(f).wait()


def last_step(at, e, w, moments):
    return pl.pallas_call(
        last_kernel,
        in_specs=[SM] + [VM] * 6,
        out_specs=HB,
        out_shape=jax.ShapeDtypeStruct((NFB, ND, ROWS, LANES), F32),
        scratch_shapes=[
            pltpu.VMEM((NFB, ND, ROWS, LANES), F32),
            pltpu.VMEM((2, ROWS, LANES), F32),
            pltpu.SemaphoreType.DMA((NFB,)),
        ],
        compiler_params=PARAMS,
        cost_estimate=cost(1.5),
        name="last_step",
    )(at, e, w, *moments)


RIGHT = [(i, (i + 1) % PTS) for i in range(PTS)]
LEFT = [(b, a) for a, b in RIGHT]


def band_parts(x):
    near, middle, far = [
        lax.ppermute(x, "band", [(i, i ^ k) for i in range(BANDS)]) for k in (1, 2, 3)
    ]
    return [x, near, far, middle]


def per_device(spectra, currents, bathymetry, sea_mask):
    forcing = jnp.concatenate(
        [
            currents.reshape(3 * SUBSTEPS, 4, LANES),
            bathymetry[None],
            sea_mask.astype(F32)[None],
        ],
        0,
    ).reshape(4 * FIELDS, LANES)
    at = jnp.stack([lax.axis_index("band"), lax.axis_index("pts")]).astype(jnp.int32)
    windows = forcing_windows(forcing)
    ml, mr = pack(jnp.transpose(spectra, (1, 2, 0, 3)))
    windows = lax.all_to_all(windows, ("band", "pts"), 0, 0, tiled=True)
    lh = lax.ppermute(mr, "pts", RIGHT)
    rh = lax.ppermute(ml, "pts", LEFT)
    turn = turns()
    lh, rh = align(at, lh, rh)
    c, u, v, w, depth = speeds(at, windows, lh)
    e, moments = first_step(at, lh, ml, mr, rh, (c, u, v, w, turn))
    c = second_speeds(at, depth)
    e, moments = second_step(at, e, band_parts(moments), c, u, v, w, turn)
    return jnp.transpose(last_step(at, unpack(e), w, band_parts(moments)), (2, 0, 1, 3))


def solution(mesh):
    in_specs = (
        P(None, "band", None, "pts"),
        P(None, None, "band", "pts"),
        P("band", "pts"),
        P("band", "pts"),
    )
    out_specs = P(None, "band", None, "pts")
    return jax.shard_map(
        per_device, mesh=mesh, in_specs=in_specs, out_specs=out_specs, check_vma=False
    )
```

```python
import math

import jax
import jax.numpy as jnp
from jax import lax
from jax.experimental import pallas as pl
from jax.experimental.pallas import tpu as pltpu
from jax.sharding import PartitionSpec as P

GRAVITY = 9.81
COURANT = 0.02
DISSIPATION = 1.0
MOMENT_FLOOR = 0.01
FREQ_FIRST = 0.035
FREQ_STEP = 1.1
BAND_WIDTH = 0.0955
ND = 36
NQ = 9
NFB = 9
ROWS = 16
BANDS = 4
PTS = 32
SUBSTEPS = 2
FIELDS = 8
LANES = 128
F32 = jnp.float32
VMEM_LIMIT = 40 * 1024 * 1024
VM = pl.BlockSpec(memory_space=pltpu.VMEM)
SM = pl.BlockSpec(memory_space=pltpu.SMEM)
HB = pl.BlockSpec(memory_space=pltpu.HBM)
PARAMS = pltpu.CompilerParams(vmem_limit_bytes=VMEM_LIMIT)


def lane_group():
    return lax.broadcasted_iota(jnp.int32, (ROWS, LANES), 1) & 3


def lroll(x, shift):
    return pltpu.roll(x, shift % LANES, 1)


def lane_swap(x, distance):
    index = lax.broadcasted_iota(jnp.int32, x.shape, 1) ^ distance
    return jnp.take_along_axis(x, index, axis=1)


def quad_transpose(a):
    lane = lane_group()

    def exchange(x, y, distance):
        low = (lane & distance) == 0
        t = lane_swap(jnp.where(low, y, x), distance)
        return jnp.where(low, x, t), jnp.where(low, t, y)

    b0, b2 = exchange(a[0], a[2], 2)
    b1, b3 = exchange(a[1], a[3], 2)
    o0, o1 = exchange(b0, b1, 1)
    o2, o3 = exchange(b2, b3, 1)
    return o0, o1, o2, o3


def quad_spread(x):
    lane = lax.broadcasted_iota(jnp.int32, x.shape, 1)
    return tuple(jnp.take_along_axis(x, (lane & ~3) + k, axis=1) for k in range(4))


def quad_sum(x):
    x = x + lane_swap(x, 1)
    return x + lane_swap(x, 2)


def select4(x):
    lane = lane_group()
    return jnp.where(
        lane < 2, jnp.where(lane == 0, x[0], x[1]), jnp.where(lane == 2, x[2], x[3])
    )


def frequency_of(index):
    return FREQ_FIRST * jnp.exp(
        jnp.full((ROWS, LANES), index, jnp.int32).astype(F32) * math.log(FREQ_STEP)
    )


def edge_shifts(pts):
    left = jnp.where(pts == 0, 4, 0)
    right = jnp.where(pts == PTS - 1, LANES - 4, 0)
    return left, right


def cost(microseconds):
    return pl.CostEstimate(
        flops=0, transcendentals=0, bytes_accessed=int(microseconds * 3.0e6)
    )


def loop(count, body):
    lax.fori_loop(0, count, lambda i, carry: (body(i), carry)[1], 0)


def load_rows(ref, lead):
    return jnp.concatenate(
        [ref[lead + (pl.ds(parity, 8, stride=2), slice(None))] for parity in range(2)], axis=0
    )


def store_rows(ref, lead, value):
    for parity in range(2):
        ref[lead + (pl.ds(parity, 8, stride=2), slice(None))] = value[8 * parity : 8 * parity + 8]


def pack_kernel(e_hbm, ml_ref, mr_ref, buf, sem):
    def load(f, h):
        part = pl.ds(18 * h, 18)
        return pltpu.make_async_copy(e_hbm.at[f, part], buf.at[f, part], sem.at[f, h])

    for f in range(NFB):
        load(f, 0).start()
        load(f, 1).start()

    def body(f):
        load(f, 0).wait()
        load(f, 1).wait()
        for d in range(NQ):
            out = quad_transpose([load_rows(buf, (f, d + NQ * q)) for q in range(4)])
            ml_ref[0, f, d] = out[0]
            ml_ref[1, f, d] = out[1]
            mr_ref[0, f, d] = out[2]
            mr_ref[1, f, d] = out[3]

    loop(NFB, body)


def pack(spectra):
    shape = jax.ShapeDtypeStruct((2, NFB, NQ, ROWS, LANES), F32)
    return pl.pallas_call(
        pack_kernel,
        in_specs=[HB],
        out_specs=[VM, VM],
        out_shape=[shape, shape],
        scratch_shapes=[
            pltpu.VMEM((NFB, ND, ROWS, LANES), F32),
            pltpu.SemaphoreType.DMA((NFB, 2)),
        ],
        compiler_params=pltpu.CompilerParams(vmem_limit_bytes=52 * 1024 * 1024),
        cost_estimate=cost(2.5),
        name="pack",
    )(spectra)


def exact_dot(a, b, dims):
    return lax.dot_general(
        a, b, (dims, ((), ())), precision=lax.Precision.HIGHEST, preferred_element_type=F32
    )


def forcing_kernel(own, out_ref):
    shape = (8 * PTS, LANES)
    place = lax.broadcasted_iota(jnp.int32, shape, 0)
    wanted = (4 * (place & (PTS - 1)) + (place >> 5) + (LANES - 2)) & (LANES - 1)
    pick = (lax.broadcasted_iota(jnp.int32, shape, 1) == wanted).astype(F32)
    x = exact_dot(pick, own[...], ((1,), (1,)))
    for h in range(2):
        row = jnp.concatenate(
            [x[PTS * (4 * h + k) : PTS * (4 * h + k) + PTS] for k in range(4)], axis=1
        )
        for band in range(BANDS):
            out_ref[PTS * band : PTS * band + PTS, h, :] = row


def forcing_windows(forcing):
    return pl.pallas_call(
        forcing_kernel,
        in_specs=[VM],
        out_specs=VM,
        out_shape=jax.ShapeDtypeStruct((BANDS * PTS, 2, LANES), F32),
        compiler_params=PARAMS,
        cost_estimate=cost(0.8),
        name="forcing",
    )(forcing)


def spread_columns(x, y):
    a, b = quad_spread(x), quad_spread(y)
    return (b[2], b[3]) + a + (b[0], b[1])


def celerities(first, h_ref, c_ref):
    for f in range(NFB):
        angular = (2.0 * math.pi) * frequency_of(first + f)
        deep = angular * angular / GRAVITY
        speed = []
        for part in range(2):
            height = h_ref[part]
            wavenumber = deep / jnp.sqrt(jnp.tanh(deep * height))
            q = 2.0 * wavenumber * height
            ratio = 2.0 * q * jnp.exp(-q) / (1.0 - jnp.exp(-2.0 * q))
            speed.append((0.5 * COURANT) * (1.0 + ratio) * angular / wavenumber)
        for i, x in enumerate(spread_columns(*speed)):
            c_ref[f, i] = x


def speed_kernel(at, win, after, c_ref, u_ref, v_ref, w_ref, h_ref, f_scr, h_scr):
    left, right = edge_shifts(at[1])
    shape = (PTS, LANES)
    place = lax.broadcasted_iota(jnp.int32, shape, 0)
    spread = ((lax.broadcasted_iota(jnp.int32, shape, 1) >> 2) == place).astype(F32)
    for band in range(BANDS):
        for h in range(2):
            block = win[PTS * band : PTS * band + PTS, h, :]
            fields = exact_dot(block, spread, ((0,), (0,)))
            for k in range(4):
                i = 4 * h + k
                part = fields[32 * k : 32 * k + 32]
                if i < 2:
                    part = pltpu.roll(part, left, 1)
                if i >= 6:
                    part = pltpu.roll(part, right, 1)
                for n in range(FIELDS):
                    f_scr[i, n, 4 * band : 4 * band + 4, :] = part[4 * n : 4 * n + 4]
    for i in range(8):
        w_ref[i] = load_rows(f_scr, (i, 7))
        for s in range(SUBSTEPS):
            u_ref[s, i] = COURANT * load_rows(f_scr, (i, 3 * s))
            v_ref[s, i] = COURANT * load_rows(f_scr, (i, 3 * s + 1))
    for s, ref in ((0, h_scr), (1, h_ref)):
        depth = [load_rows(f_scr, (i, 6)) + load_rows(f_scr, (i, 3 * s + 2)) for i in range(8)]
        ref[0] = select4(depth[2:6])
        ref[1] = select4([depth[6], depth[7], depth[0], depth[1]])
    celerities(at[0] * NFB, h_scr, c_ref)


def speeds(at, windows, after):
    return pl.pallas_call(
        speed_kernel,
        in_specs=[SM, VM, pl.BlockSpec(memory_space=pl.ANY)],
        out_specs=[VM] * 5,
        out_shape=[
            jax.ShapeDtypeStruct((NFB, 8, ROWS, LANES), F32),
            jax.ShapeDtypeStruct((SUBSTEPS, 8, ROWS, LANES), F32),
            jax.ShapeDtypeStruct((SUBSTEPS, 8, ROWS, LANES), F32),
            jax.ShapeDtypeStruct((8, ROWS, LANES), F32),
            jax.ShapeDtypeStruct((2, ROWS, LANES), F32),
        ],
        scratch_shapes=[
            pltpu.VMEM((8, FIELDS, ROWS, LANES), F32),
            pltpu.VMEM((2, ROWS, LANES), F32),
        ],
        compiler_params=PARAMS,
        cost_estimate=cost(2.0),
        name="speeds",
    )(at, windows, after)


def turn_kernel(t_ref):
    for d in range(NQ):
        angle = (d + NQ * lane_group()[0:8]).astype(F32) * (2.0 * math.pi / ND)
        t_ref[0, d] = jnp.cos(angle)
        t_ref[1, d] = jnp.sin(angle)


def turns():
    return pl.pallas_call(
        turn_kernel,
        out_specs=VM,
        out_shape=jax.ShapeDtypeStruct((2, NQ, 8, LANES), F32),
        compiler_params=PARAMS,
        cost_estimate=cost(0.5),
        name="turns",
    )()


def align_kernel(at, lh, rh, lo_ref, ro_ref):
    def shift(ref, amount):
        def body(f):
            for k in range(2):
                for d in range(NQ):
                    ref[k, f, d] = lroll(ref[k, f, d], amount)

        loop(NFB, body)

    @pl.when(at[1] == 0)
    def _():
        shift(lo_ref, 4)

    @pl.when(at[1] == PTS - 1)
    def _():
        shift(ro_ref, -4)


def align(at, lh, rh):
    shape = jax.ShapeDtypeStruct((2, NFB, NQ, ROWS, LANES), F32)
    return pl.pallas_call(
        align_kernel,
        in_specs=[SM, VM, VM],
        out_specs=[VM, VM],
        out_shape=[shape, shape],
        input_output_aliases={1: 0, 2: 1},
        compiler_params=PARAMS,
        cost_estimate=cost(1.0),
        name="align",
    )(at, lh, rh)


def second_speed_kernel(at, h_ref, c_ref):
    celerities(at[0] * NFB, h_ref, c_ref)


def second_speeds(at, h):
    return pl.pallas_call(
        second_speed_kernel,
        in_specs=[SM, VM],
        out_specs=VM,
        out_shape=jax.ShapeDtypeStruct((NFB, 8, ROWS, LANES), F32),
        compiler_params=PARAMS,
        cost_estimate=cost(1.5),
        name="second_speeds",
    )(at, h)


def row_flux(b):
    sub = lax.broadcasted_iota(jnp.int32, (8, LANES), 0)
    plus, minus = jnp.maximum(b, 0.0), jnp.minimum(b, 0.0)
    even = plus[0:8] + minus[8:16]
    odd = plus[8:16] + jnp.where(sub == 7, 0.0, pltpu.roll(minus[0:8], 7, 0))
    before = jnp.where(sub == 0, minus[0:8], pltpu.roll(odd, 1, 0))
    return jnp.concatenate([even - before, odd - even], axis=0)


def advance(count, energy, speed, current_x, current_y, cos, sin, store):
    plus = None
    entered = None
    part = None
    for i in range(count):
        e = energy(i)
        c = speed(i)
        a = (c * cos + current_x(i)) * e
        if plus is not None:
            crossed = plus + jnp.minimum(a, 0.0)
            if part is not None:
                store(i - 1, part - crossed)
            entered = crossed
        if 0 < i < count - 1:
            b = (c * sin + current_y(i)) * e
            part = e + entered - row_flux(b)
        plus = jnp.maximum(a, 0.0)


UNROLL = 9


def zeros(count):
    return tuple(jnp.zeros((ROWS, LANES), F32) for _ in range(count))


def twice(x):
    return jnp.concatenate([x, x], axis=0)


def add_moments(acc, levels, wet, freq):
    weight = (BAND_WIDTH * (2.0 * math.pi / ND)) * freq
    for i, level in enumerate(levels):
        t = level * wet(i) * weight
        acc[0, i] = acc[0, i] + t
        acc[1, i] = acc[1, i] + t * freq


def first_kernel(at, lh, ml, mr, rh, c_ref, u_ref, v_ref, w_ref, t_ref, out_ref, mom_ref, acc):
    first = at[0] * NFB
    acc[...] = jnp.zeros_like(acc)

    def body(f):
        def over(d, levels):
            levels = list(levels)

            def store(i, value):
                out_ref[i - 1, f, d] = value
                levels[i - 1] = levels[i - 1] + value

            def energy(i):
                return (lh, ml, mr, rh)[i // 2][i % 2, f, d] * w_ref[i]

            advance(
                8,
                energy,
                lambda i: c_ref[f, i],
                lambda i: u_ref[0, i],
                lambda i: v_ref[0, i],
                twice(t_ref[0, d]),
                twice(t_ref[1, d]),
                store,
            )
            return tuple(levels)

        levels = lax.fori_loop(0, NQ, over, zeros(6), unroll=UNROLL)
        add_moments(acc, levels, lambda i: w_ref[i + 1], frequency_of(first + f))

    loop(NFB, body)
    for m in range(2):
        sums = [quad_sum(acc[m, i]) for i in range(6)]
        mom_ref[m, 0] = select4(sums[1:5])
        mom_ref[m, 1] = jnp.where(lane_group() < 2, sums[0], sums[5])


def first_step(at, lh, ml, mr, rh, tables):
    return pl.pallas_call(
        first_kernel,
        in_specs=[SM] + [VM] * 9,
        out_specs=[VM] * 2,
        out_shape=[
            jax.ShapeDtypeStruct((6, NFB, NQ, ROWS, LANES), F32),
            jax.ShapeDtypeStruct((2, 2, ROWS, LANES), F32),
        ],
        scratch_shapes=[pltpu.VMEM((2, 6, ROWS, LANES), F32)],
        compiler_params=PARAMS,
        cost_estimate=cost(5.0),
        name="first_step",
    )(at, lh, ml, mr, rh, *tables)


def strength_of(parts, k):
    def total(m):
        a = [p[(m,) + k] for p in parts]
        return (a[0] + a[1]) + (a[2] + a[3])

    zeroth, first_moment = total(0), total(1)
    return DISSIPATION * zeroth * (first_moment / jnp.maximum(zeroth, MOMENT_FLOOR))


def second_kernel(
    at, e_ref, m0, m1, m2, m3, c_ref, u_ref, v_ref, w_ref, t_ref,
    out_ref, mom_ref, acc, s_scr, d_scr,
):
    first = at[0] * NFB
    acc[...] = jnp.zeros_like(acc)
    own = quad_spread(strength_of((m0, m1, m2, m3), (0,)))
    edge = quad_spread(strength_of((m0, m1, m2, m3), (1,)))
    for i, x in enumerate((edge[0],) + own + (edge[2],)):
        s_scr[i] = x

    def body(f, carry):
        freq = frequency_of(first + f)
        square = freq * freq
        for i in range(6):
            d_scr[i] = w_ref[i + 1] / (1.0 + s_scr[i] * square)
        def over(d, levels):
            levels = list(levels)

            def store(i, value):
                out_ref[i - 1, f, d] = value
                levels[i - 1] = levels[i - 1] + value

            advance(
                6,
                lambda i: e_ref[i, f, d] * d_scr[i],
                lambda i: c_ref[f, i + 1],
                lambda i: u_ref[1, i + 1],
                lambda i: v_ref[1, i + 1],
                twice(t_ref[0, d]),
                twice(t_ref[1, d]),
                store,
            )
            return tuple(levels)

        levels = lax.fori_loop(0, NQ, over, zeros(4), unroll=UNROLL)
        add_moments(acc, levels, lambda i: w_ref[i + 2], freq)
        return carry

    lax.fori_loop(0, NFB, body, 0)
    for m in range(2):
        mom_ref[m] = select4([quad_sum(acc[m, i]) for i in range(4)])


def second_step(at, e, moments, c, u, v, w, t):
    return pl.pallas_call(
        second_kernel,
        in_specs=[SM] + [VM] * 10,
        out_specs=[VM] * 2,
        out_shape=[
            jax.ShapeDtypeStruct((4, NFB, NQ, ROWS, LANES), F32),
            jax.ShapeDtypeStruct((2, ROWS, LANES), F32),
        ],
        scratch_shapes=[
            pltpu.VMEM((2, 4, ROWS, LANES), F32),
            pltpu.VMEM((6, ROWS, LANES), F32),
            pltpu.VMEM((6, ROWS, LANES), F32),
        ],
        compiler_params=PARAMS,
        cost_estimate=cost(3.5),
        name="second_step",
    )(at, e, *moments, c, u, v, w, t)


def unpack_kernel(e_ref, out_ref):
    def body(f, carry):
        for d in range(NQ):
            out = quad_transpose([e_ref[c, f, d] for c in range(4)])
            for q in range(4):
                store_rows(out_ref, (f, d + NQ * q), out[q])
        return carry

    lax.fori_loop(0, NFB, body, 0)


def unpack(e):
    return pl.pallas_call(
        unpack_kernel,
        in_specs=[VM],
        out_specs=VM,
        out_shape=jax.ShapeDtypeStruct((NFB, ND, ROWS, LANES), F32),
        compiler_params=PARAMS,
        cost_estimate=cost(2.0),
        name="unpack",
    )(e)


def last_kernel(at, e_ref, w_ref, m0, m1, m2, m3, out_hbm, buf, s_scr, sem):
    first = at[0] * NFB
    store_rows(s_scr, (0,), strength_of((m0, m1, m2, m3), ()))
    store_rows(s_scr, (1,), select4([w_ref[i] for i in range(2, 6)]))

    def save(f):
        return pltpu.make_async_copy(buf.at[f], out_hbm.at[f], sem.at[f])

    def body(f, carry):
        freq = frequency_of(first + f)
        damp = s_scr[1] / (1.0 + s_scr[0] * (freq * freq))
        for d in range(ND):
            buf[f, d] = e_ref[f, d] * damp
        save(f).start()
        return carry

    lax.fori_loop(0, NFB, body, 0)
    for f in range(NFB):
        save(f).wait()


def last_step(at, e, w, moments):
    return pl.pallas_call(
        last_kernel,
        in_specs=[SM] + [VM] * 6,
        out_specs=HB,
        out_shape=jax.ShapeDtypeStruct((NFB, ND, ROWS, LANES), F32),
        scratch_shapes=[
            pltpu.VMEM((NFB, ND, ROWS, LANES), F32),
            pltpu.VMEM((2, ROWS, LANES), F32),
            pltpu.SemaphoreType.DMA((NFB,)),
        ],
        compiler_params=PARAMS,
        cost_estimate=cost(1.5),
        name="last_step",
    )(at, e, w, *moments)


RIGHT = [(i, (i + 1) % PTS) for i in range(PTS)]
LEFT = [(b, a) for a, b in RIGHT]


def band_parts(x):
    near, middle, far = [
        lax.ppermute(x, "band", [(i, i ^ k) for i in range(BANDS)]) for k in (1, 2, 3)
    ]
    return [x, near, far, middle]


def per_device(spectra, currents, bathymetry, sea_mask):
    forcing = jnp.concatenate(
        [
            currents.reshape(3 * SUBSTEPS, 4, LANES),
            bathymetry[None],
            sea_mask.astype(F32)[None],
        ],
        0,
    ).reshape(4 * FIELDS, LANES)
    at = jnp.stack([lax.axis_index("band"), lax.axis_index("pts")]).astype(jnp.int32)
    windows = forcing_windows(forcing)
    ml, mr = pack(jnp.transpose(spectra, (1, 2, 0, 3)))
    windows = lax.all_to_all(windows, ("band", "pts"), 0, 0, tiled=True)
    lh = lax.ppermute(mr, "pts", RIGHT)
    rh = lax.ppermute(ml, "pts", LEFT)
    turn = turns()
    lh, rh = align(at, lh, rh)
    c, u, v, w, depth = speeds(at, windows, lh)
    e, moments = first_step(at, lh, ml, mr, rh, (c, u, v, w, turn))
    c = second_speeds(at, depth)
    e, moments = second_step(at, e, band_parts(moments), c, u, v, w, turn)
    return jnp.transpose(last_step(at, unpack(e), w, band_parts(moments)), (2, 0, 1, 3))


def solution(mesh):
    in_specs = (
        P(None, "band", None, "pts"),
        P(None, None, "band", "pts"),
        P("band", "pts"),
        P("band", "pts"),
    )
    out_specs = P(None, "band", None, "pts")
    return jax.shard_map(
        per_device, mesh=mesh, in_specs=in_specs, out_specs=out_specs, check_vma=False
    )
```

```python
import math

import jax
import jax.numpy as jnp
from jax import lax
from jax.experimental import pallas as pl
from jax.experimental.pallas import tpu as pltpu
from jax.sharding import PartitionSpec as P

GRAVITY = 9.81
COURANT = 0.02
DISSIPATION = 1.0
MOMENT_FLOOR = 0.01
FREQ_FIRST = 0.035
FREQ_STEP = 1.1
BAND_WIDTH = 0.0955
ND = 36
NQ = 9
NFB = 9
ROWS = 16
BANDS = 4
PTS = 32
SUBSTEPS = 2
FIELDS = 8
LANES = 128
F32 = jnp.float32
VMEM_LIMIT = 24 * 1024 * 1024
VM = pl.BlockSpec(memory_space=pltpu.VMEM)
SM = pl.BlockSpec(memory_space=pltpu.SMEM)
HB = pl.BlockSpec(memory_space=pltpu.HBM)
PARAMS = pltpu.CompilerParams(vmem_limit_bytes=VMEM_LIMIT)


def lane_group():
    return lax.broadcasted_iota(jnp.int32, (ROWS, LANES), 1) & 3


def lroll(x, shift):
    return pltpu.roll(x, shift % LANES, 1)


def lane_swap(x, distance):
    index = lax.broadcasted_iota(jnp.int32, x.shape, 1) ^ distance
    return jnp.take_along_axis(x, index, axis=1)


def quad_transpose(a):
    lane = lane_group()

    def exchange(x, y, distance):
        low = (lane & distance) == 0
        t = lane_swap(jnp.where(low, y, x), distance)
        return jnp.where(low, x, t), jnp.where(low, t, y)

    b0, b2 = exchange(a[0], a[2], 2)
    b1, b3 = exchange(a[1], a[3], 2)
    o0, o1 = exchange(b0, b1, 1)
    o2, o3 = exchange(b2, b3, 1)
    return o0, o1, o2, o3


def quad_spread(x):
    lane = lax.broadcasted_iota(jnp.int32, x.shape, 1)
    return tuple(jnp.take_along_axis(x, (lane & ~3) + k, axis=1) for k in range(4))


def quad_sum(x):
    x = x + lane_swap(x, 1)
    return x + lane_swap(x, 2)


def select4(x):
    lane = lane_group()
    return jnp.where(
        lane < 2, jnp.where(lane == 0, x[0], x[1]), jnp.where(lane == 2, x[2], x[3])
    )


def frequency_of(index):
    return FREQ_FIRST * jnp.exp(
        jnp.full((ROWS, LANES), index, jnp.int32).astype(F32) * math.log(FREQ_STEP)
    )


def edge_shifts(pts):
    left = jnp.where(pts == 0, 4, 0)
    right = jnp.where(pts == PTS - 1, LANES - 4, 0)
    return left, right


def cost(microseconds):
    return pl.CostEstimate(
        flops=0, transcendentals=0, bytes_accessed=int(microseconds * 3.0e6)
    )


def loop(count, body):
    lax.fori_loop(0, count, lambda i, carry: (body(i), carry)[1], 0)


def load_rows(ref, lead):
    return jnp.concatenate(
        [ref[lead + (pl.ds(parity, 8, stride=2), slice(None))] for parity in range(2)], axis=0
    )


def store_rows(ref, lead, value):
    for parity in range(2):
        ref[lead + (pl.ds(parity, 8, stride=2), slice(None))] = value[8 * parity : 8 * parity + 8]


def pack_kernel(e_hbm, ml_ref, mr_ref, buf, sem):
    def load(f):
        return pltpu.make_async_copy(e_hbm.at[f], buf.at[f], sem.at[f])

    for f in range(NFB):
        load(f).start()

    def body(f):
        load(f).wait()
        for d in range(NQ):
            out = quad_transpose([load_rows(buf, (f, d + NQ * q)) for q in range(4)])
            ml_ref[0, f, d] = out[0]
            ml_ref[1, f, d] = out[1]
            mr_ref[0, f, d] = out[2]
            mr_ref[1, f, d] = out[3]

    loop(NFB, body)


def pack(spectra):
    shape = jax.ShapeDtypeStruct((2, NFB, NQ, ROWS, LANES), F32)
    return pl.pallas_call(
        pack_kernel,
        in_specs=[HB],
        out_specs=[VM, VM],
        out_shape=[shape, shape],
        scratch_shapes=[
            pltpu.VMEM((NFB, ND, ROWS, LANES), F32),
            pltpu.SemaphoreType.DMA((NFB,)),
        ],
        compiler_params=pltpu.CompilerParams(vmem_limit_bytes=52 * 1024 * 1024),
        cost_estimate=cost(2.5),
        name="pack",
    )(spectra)


def exact_dot(a, b, dims):
    return lax.dot_general(
        a, b, (dims, ((), ())), precision=lax.Precision.HIGHEST, preferred_element_type=F32
    )


def forcing_kernel(own, out_ref):
    shape = (8 * PTS, LANES)
    place = lax.broadcasted_iota(jnp.int32, shape, 0)
    wanted = (4 * (place & (PTS - 1)) + (place >> 5) + (LANES - 2)) & (LANES - 1)
    pick = (lax.broadcasted_iota(jnp.int32, shape, 1) == wanted).astype(F32)
    x = exact_dot(pick, own[...], ((1,), (1,)))
    for h in range(2):
        row = jnp.concatenate(
            [x[PTS * (4 * h + k) : PTS * (4 * h + k) + PTS] for k in range(4)], axis=1
        )
        for band in range(BANDS):
            out_ref[PTS * band : PTS * band + PTS, h, :] = row


def forcing_windows(forcing):
    return pl.pallas_call(
        forcing_kernel,
        in_specs=[VM],
        out_specs=VM,
        out_shape=jax.ShapeDtypeStruct((BANDS * PTS, 2, LANES), F32),
        compiler_params=PARAMS,
        cost_estimate=cost(0.8),
        name="forcing",
    )(forcing)


def spread_columns(x, y):
    a, b = quad_spread(x), quad_spread(y)
    return (b[2], b[3]) + a + (b[0], b[1])


def celerities(first, h_ref, c_ref):
    for f in range(NFB):
        angular = (2.0 * math.pi) * frequency_of(first + f)
        deep = angular * angular / GRAVITY
        speed = []
        for part in range(2):
            height = h_ref[part]
            wavenumber = deep / jnp.sqrt(jnp.tanh(deep * height))
            q = 2.0 * wavenumber * height
            ratio = 2.0 * q * jnp.exp(-q) / (1.0 - jnp.exp(-2.0 * q))
            speed.append((0.5 * COURANT) * (1.0 + ratio) * angular / wavenumber)
        for i, x in enumerate(spread_columns(*speed)):
            c_ref[f, i] = x


def speed_kernel(at, win, after, c_ref, u_ref, v_ref, w_ref, h_ref, f_scr, h_scr):
    left, right = edge_shifts(at[1])
    shape = (PTS, LANES)
    place = lax.broadcasted_iota(jnp.int32, shape, 0)
    spread = ((lax.broadcasted_iota(jnp.int32, shape, 1) >> 2) == place).astype(F32)
    for band in range(BANDS):
        for h in range(2):
            block = win[PTS * band : PTS * band + PTS, h, :]
            fields = exact_dot(block, spread, ((0,), (0,)))
            for k in range(4):
                i = 4 * h + k
                part = fields[32 * k : 32 * k + 32]
                if i < 2:
                    part = pltpu.roll(part, left, 1)
                if i >= 6:
                    part = pltpu.roll(part, right, 1)
                for n in range(FIELDS):
                    f_scr[i, n, 4 * band : 4 * band + 4, :] = part[4 * n : 4 * n + 4]
    for i in range(8):
        w_ref[i] = load_rows(f_scr, (i, 7))
        for s in range(SUBSTEPS):
            u_ref[s, i] = COURANT * load_rows(f_scr, (i, 3 * s))
            v_ref[s, i] = COURANT * load_rows(f_scr, (i, 3 * s + 1))
    for s, ref in ((0, h_scr), (1, h_ref)):
        depth = [load_rows(f_scr, (i, 6)) + load_rows(f_scr, (i, 3 * s + 2)) for i in range(8)]
        ref[0] = select4(depth[2:6])
        ref[1] = select4([depth[6], depth[7], depth[0], depth[1]])
    celerities(at[0] * NFB, h_scr, c_ref)


def speeds(at, windows, after):
    return pl.pallas_call(
        speed_kernel,
        in_specs=[SM, VM, pl.BlockSpec(memory_space=pl.ANY)],
        out_specs=[VM] * 5,
        out_shape=[
            jax.ShapeDtypeStruct((NFB, 8, ROWS, LANES), F32),
            jax.ShapeDtypeStruct((SUBSTEPS, 8, ROWS, LANES), F32),
            jax.ShapeDtypeStruct((SUBSTEPS, 8, ROWS, LANES), F32),
            jax.ShapeDtypeStruct((8, ROWS, LANES), F32),
            jax.ShapeDtypeStruct((2, ROWS, LANES), F32),
        ],
        scratch_shapes=[
            pltpu.VMEM((8, FIELDS, ROWS, LANES), F32),
            pltpu.VMEM((2, ROWS, LANES), F32),
        ],
        compiler_params=PARAMS,
        cost_estimate=cost(2.0),
        name="speeds",
    )(at, windows, after)


def turn_kernel(t_ref):
    for d in range(NQ):
        angle = (d + NQ * lane_group()[0:8]).astype(F32) * (2.0 * math.pi / ND)
        t_ref[0, d] = jnp.cos(angle)
        t_ref[1, d] = jnp.sin(angle)


def turns():
    return pl.pallas_call(
        turn_kernel,
        out_specs=VM,
        out_shape=jax.ShapeDtypeStruct((2, NQ, 8, LANES), F32),
        compiler_params=PARAMS,
        cost_estimate=cost(0.5),
        name="turns",
    )()


def align_kernel(at, lh, rh, lo_ref, ro_ref):
    def shift(ref, amount):
        def body(f):
            for k in range(2):
                for d in range(NQ):
                    ref[k, f, d] = lroll(ref[k, f, d], amount)

        loop(NFB, body)

    @pl.when(at[1] == 0)
    def _():
        shift(lo_ref, 4)

    @pl.when(at[1] == PTS - 1)
    def _():
        shift(ro_ref, -4)


def align(at, lh, rh):
    shape = jax.ShapeDtypeStruct((2, NFB, NQ, ROWS, LANES), F32)
    return pl.pallas_call(
        align_kernel,
        in_specs=[SM, VM, VM],
        out_specs=[VM, VM],
        out_shape=[shape, shape],
        input_output_aliases={1: 0, 2: 1},
        compiler_params=PARAMS,
        cost_estimate=cost(1.0),
        name="align",
    )(at, lh, rh)


def second_speed_kernel(at, h_ref, c_ref):
    celerities(at[0] * NFB, h_ref, c_ref)


def second_speeds(at, h):
    return pl.pallas_call(
        second_speed_kernel,
        in_specs=[SM, VM],
        out_specs=VM,
        out_shape=jax.ShapeDtypeStruct((NFB, 8, ROWS, LANES), F32),
        compiler_params=PARAMS,
        cost_estimate=cost(1.5),
        name="second_speeds",
    )(at, h)


def row_flux(b):
    sub = lax.broadcasted_iota(jnp.int32, (8, LANES), 0)
    plus, minus = jnp.maximum(b, 0.0), jnp.minimum(b, 0.0)
    even = plus[0:8] + minus[8:16]
    odd = plus[8:16] + jnp.where(sub == 7, 0.0, pltpu.roll(minus[0:8], 7, 0))
    before = jnp.where(sub == 0, minus[0:8], pltpu.roll(odd, 1, 0))
    return jnp.concatenate([even - before, odd - even], axis=0)


def advance(count, energy, speed, current_x, current_y, cos, sin, store):
    plus = None
    entered = None
    part = None
    for i in range(count):
        e = energy(i)
        c = speed(i)
        a = (c * cos + current_x(i)) * e
        if plus is not None:
            crossed = plus + jnp.minimum(a, 0.0)
            if part is not None:
                store(i - 1, part - crossed)
            entered = crossed
        if 0 < i < count - 1:
            b = (c * sin + current_y(i)) * e
            part = e + entered - row_flux(b)
        plus = jnp.maximum(a, 0.0)


UNROLL = 9


def zeros(count):
    return tuple(jnp.zeros((ROWS, LANES), F32) for _ in range(count))


def twice(x):
    return jnp.concatenate([x, x], axis=0)


def add_moments(acc, levels, wet, freq):
    weight = (BAND_WIDTH * (2.0 * math.pi / ND)) * freq
    for i, level in enumerate(levels):
        t = level * wet(i) * weight
        acc[0, i] = acc[0, i] + t
        acc[1, i] = acc[1, i] + t * freq


def first_kernel(at, lh, ml, mr, rh, c_ref, u_ref, v_ref, w_ref, t_ref, out_ref, mom_ref, acc):
    first = at[0] * NFB
    acc[...] = jnp.zeros_like(acc)

    def body(f):
        def over(d, levels):
            levels = list(levels)

            def store(i, value):
                out_ref[i - 1, f, d] = value
                levels[i - 1] = levels[i - 1] + value

            def energy(i):
                return (lh, ml, mr, rh)[i // 2][i % 2, f, d] * w_ref[i]

            advance(
                8,
                energy,
                lambda i: c_ref[f, i],
                lambda i: u_ref[0, i],
                lambda i: v_ref[0, i],
                twice(t_ref[0, d]),
                twice(t_ref[1, d]),
                store,
            )
            return tuple(levels)

        levels = lax.fori_loop(0, NQ, over, zeros(6), unroll=UNROLL)
        add_moments(acc, levels, lambda i: w_ref[i + 1], frequency_of(first + f))

    loop(NFB, body)
    for m in range(2):
        sums = [quad_sum(acc[m, i]) for i in range(6)]
        mom_ref[m, 0] = select4(sums[1:5])
        mom_ref[m, 1] = jnp.where(lane_group() < 2, sums[0], sums[5])


def first_step(at, lh, ml, mr, rh, tables):
    return pl.pallas_call(
        first_kernel,
        in_specs=[SM] + [VM] * 9,
        out_specs=[VM] * 2,
        out_shape=[
            jax.ShapeDtypeStruct((6, NFB, NQ, ROWS, LANES), F32),
            jax.ShapeDtypeStruct((2, 2, ROWS, LANES), F32),
        ],
        scratch_shapes=[pltpu.VMEM((2, 6, ROWS, LANES), F32)],
        compiler_params=PARAMS,
        cost_estimate=cost(5.0),
        name="first_step",
    )(at, lh, ml, mr, rh, *tables)


def strength_of(parts, k):
    def total(m):
        a = [p[(m,) + k] for p in parts]
        return (a[0] + a[1]) + (a[2] + a[3])

    zeroth, first_moment = total(0), total(1)
    return DISSIPATION * zeroth * (first_moment / jnp.maximum(zeroth, MOMENT_FLOOR))


def second_kernel(
    at, e_ref, m0, m1, m2, m3, c_ref, u_ref, v_ref, w_ref, t_ref,
    out_ref, mom_ref, acc, s_scr, d_scr,
):
    first = at[0] * NFB
    acc[...] = jnp.zeros_like(acc)
    own = quad_spread(strength_of((m0, m1, m2, m3), (0,)))
    edge = quad_spread(strength_of((m0, m1, m2, m3), (1,)))
    for i, x in enumerate((edge[0],) + own + (edge[2],)):
        s_scr[i] = x

    def body(f, carry):
        freq = frequency_of(first + f)
        square = freq * freq
        for i in range(6):
            d_scr[i] = w_ref[i + 1] / (1.0 + s_scr[i] * square)
        def over(d, levels):
            levels = list(levels)

            def store(i, value):
                out_ref[i - 1, f, d] = value
                levels[i - 1] = levels[i - 1] + value

            advance(
                6,
                lambda i: e_ref[i, f, d] * d_scr[i],
                lambda i: c_ref[f, i + 1],
                lambda i: u_ref[1, i + 1],
                lambda i: v_ref[1, i + 1],
                twice(t_ref[0, d]),
                twice(t_ref[1, d]),
                store,
            )
            return tuple(levels)

        levels = lax.fori_loop(0, NQ, over, zeros(4), unroll=UNROLL)
        add_moments(acc, levels, lambda i: w_ref[i + 2], freq)
        return carry

    lax.fori_loop(0, NFB, body, 0)
    for m in range(2):
        mom_ref[m] = select4([quad_sum(acc[m, i]) for i in range(4)])


def second_step(at, e, moments, c, u, v, w, t):
    return pl.pallas_call(
        second_kernel,
        in_specs=[SM] + [VM] * 10,
        out_specs=[VM] * 2,
        out_shape=[
            jax.ShapeDtypeStruct((4, NFB, NQ, ROWS, LANES), F32),
            jax.ShapeDtypeStruct((2, ROWS, LANES), F32),
        ],
        scratch_shapes=[
            pltpu.VMEM((2, 4, ROWS, LANES), F32),
            pltpu.VMEM((6, ROWS, LANES), F32),
            pltpu.VMEM((6, ROWS, LANES), F32),
        ],
        compiler_params=PARAMS,
        cost_estimate=cost(3.5),
        name="second_step",
    )(at, e, *moments, c, u, v, w, t)


def unpack_kernel(e_ref, out_ref):
    def body(f, carry):
        for d in range(NQ):
            out = quad_transpose([e_ref[c, f, d] for c in range(4)])
            for q in range(4):
                store_rows(out_ref, (f, d + NQ * q), out[q])
        return carry

    lax.fori_loop(0, NFB, body, 0)


def unpack(e):
    return pl.pallas_call(
        unpack_kernel,
        in_specs=[VM],
        out_specs=VM,
        out_shape=jax.ShapeDtypeStruct((NFB, ND, ROWS, LANES), F32),
        compiler_params=PARAMS,
        cost_estimate=cost(2.0),
        name="unpack",
    )(e)


def last_kernel(at, e_ref, w_ref, m0, m1, m2, m3, out_hbm, buf, s_scr, sem):
    first = at[0] * NFB
    store_rows(s_scr, (0,), strength_of((m0, m1, m2, m3), ()))
    store_rows(s_scr, (1,), select4([w_ref[i] for i in range(2, 6)]))

    def save(f):
        return pltpu.make_async_copy(buf.at[f], out_hbm.at[f], sem.at[f])

    def body(f, carry):
        freq = frequency_of(first + f)
        damp = s_scr[1] / (1.0 + s_scr[0] * (freq * freq))
        for d in range(ND):
            buf[f, d] = e_ref[f, d] * damp
        save(f).start()
        return carry

    lax.fori_loop(0, NFB, body, 0)
    for f in range(NFB):
        save(f).wait()


def last_step(at, e, w, moments):
    return pl.pallas_call(
        last_kernel,
        in_specs=[SM] + [VM] * 6,
        out_specs=HB,
        out_shape=jax.ShapeDtypeStruct((NFB, ND, ROWS, LANES), F32),
        scratch_shapes=[
            pltpu.VMEM((NFB, ND, ROWS, LANES), F32),
            pltpu.VMEM((2, ROWS, LANES), F32),
            pltpu.SemaphoreType.DMA((NFB,)),
        ],
        compiler_params=PARAMS,
        cost_estimate=cost(1.5),
        name="last_step",
    )(at, e, w, *moments)


RIGHT = [(i, (i + 1) % PTS) for i in range(PTS)]
LEFT = [(b, a) for a, b in RIGHT]


def band_parts(x):
    near, middle, far = [
        lax.ppermute(x, "band", [(i, i ^ k) for i in range(BANDS)]) for k in (1, 2, 3)
    ]
    return [x, near, far, middle]


def per_device(spectra, currents, bathymetry, sea_mask):
    forcing = jnp.concatenate(
        [
            currents.reshape(3 * SUBSTEPS, 4, LANES),
            bathymetry[None],
            sea_mask.astype(F32)[None],
        ],
        0,
    ).reshape(4 * FIELDS, LANES)
    at = jnp.stack([lax.axis_index("band"), lax.axis_index("pts")]).astype(jnp.int32)
    windows = forcing_windows(forcing)
    ml, mr = pack(jnp.transpose(spectra, (1, 2, 0, 3)))
    windows = lax.all_to_all(windows, ("band", "pts"), 0, 0, tiled=True)
    lh = lax.ppermute(mr, "pts", RIGHT)
    rh = lax.ppermute(ml, "pts", LEFT)
    turn = turns()
    lh, rh = align(at, lh, rh)
    c, u, v, w, depth = speeds(at, windows, lh)
    e, moments = first_step(at, lh, ml, mr, rh, (c, u, v, w, turn))
    c = second_speeds(at, depth)
    e, moments = second_step(at, e, band_parts(moments), c, u, v, w, turn)
    return jnp.transpose(last_step(at, unpack(e), w, band_parts(moments)), (2, 0, 1, 3))


def solution(mesh):
    in_specs = (
        P(None, "band", None, "pts"),
        P(None, None, "band", "pts"),
        P("band", "pts"),
        P("band", "pts"),
    )
    out_specs = P(None, "band", None, "pts")
    return jax.shard_map(
        per_device, mesh=mesh, in_specs=in_specs, out_specs=out_specs, check_vma=False
    )
```
